256 devices in a mesh: section: 8 (over z), ep: 32 (over y, x, core).
Axes of the slice: x: 4, y: 4, z: 8, core: 2. Of those that a mesh axis runs over, the one named last changes fastest.
Arguments:
- arriving: bfloat16 [8, 2048, 3072], P('section', 'ep'), may hold values from -6 to 6
- top_grad: bfloat16 [1, 2048, 3072], P(None, 'ep'), may hold values from -6 to 6
- expert_ids: int32 [8, 2, 2048, 2], P('section'), may hold values from 0 to 3, all different within a row; in each aligned block of 64 rows (0 to 63, 64 to 127, ..., all dimensions but the last counted through in order) at most 36 rows name the same one
- first_share: float32 [8, 2, 2048], P('section', None, 'ep'), may hold values from 0.5 to 0.95
- out_gap: bfloat16 [8, 2, 2048, 3072], P('section', None, 'ep'), may hold values from -6 to 6
- router_weight: float32 [8, 4, 3072], P('section'), may hold values from -0.75 to 0.75
- down_weight: bfloat16 [8, 32768, 3072], P('section', 'ep'), may hold values from -0.109375 to 0.109375
Outputs:
- departing: bfloat16 [8, 2, 2048, 3072], P('section', None, 'ep')
- hidden_grad: bfloat16 [8, 2, 36864, 1024], P('section', None, 'ep')
The draws below stay inside these ranges and needn't reach their ends.
Inputs may be any that keep to these rules, and one draw needn't show every extreme that they name: `expert_ids`: A token's two ids differ; within one step each device's 64 tokens name any one expert at most 36 times.
All inputs are finite; a program needn't handle non-finite values.
Results may differ from the reference program's by a relative error of at most 0.0054.
Values may be sent and summed in bfloat16 or wider, within the bound.
No kernel may reach another device: no remote copies, remote signals or barrier semaphores. Data moves between devices by JAX's collectives and lax.ppermute only.
A program may use at most 128 MiB of HBM per device.

```python
import math
import jax
import jax.numpy as jnp
import numpy as np
from jax import lax

D = 3072
FF = 8192
EXPERTS = 4
MB_DEV = 64
TICKS = 2
CAP = 36
GROUP = 8
HID_DEV = 1024
MAXP = 1152
TOKENS = 2048
N_SECTION = 8
N_EP = 32


def level_of(own_key, extent, shards, least, high):
    def one(axis_at, parts):
        steps = jax.random.uniform(jax.random.fold_in(jax.random.fold_in(own_key, 6), axis_at), (parts,), jnp.float32, least / len(shards), high / len(shards))
        return jnp.repeat(jnp.exp(steps), extent[axis_at] // parts).reshape((-1,) + (1,) * (len(extent) - axis_at - 1))

    factor_of = one(*shards[0])
    for cut in shards[1:]:
        factor_of = factor_of * one(*cut)
    return factor_of


def assign_block(rng, own, number, rows, amount, top, limit, skew):
    ranking = jax.random.permutation(rng, amount)
    crowded, common = shares(amount, rows * top, limit, skew, True), shares(amount, rows * top, limit, skew, False)
    places = jnp.arange(amount)

    def named(sizes, turn):
        used = int((sizes > 0).sum())
        fixed = max(1, used // 4)
        shifted = fixed + (places - fixed + turn * (used - fixed)) % max(1, amount - fixed)
        return jnp.zeros((amount,), jnp.int32).at[ranking[jnp.where(places < fixed, places, shifted)]].set(jnp.asarray(sizes, jnp.int32))

    sizes = jnp.where(number % 4 == 0, named(crowded, number // 4), named(common, number - number // 4 - 1))
    mixed = jax.random.permutation(jax.random.fold_in(own, 3), amount)
    source_of, sink = mixed[0:amount // 2 * 2:2], mixed[1:amount // 2 * 2:2]
    margin = jnp.minimum(sizes[source_of] - 1, limit - sizes[sink]) // 2
    margin = jnp.where((source_of == ranking[0]) | (sink == ranking[0]) | (sizes[sink] == 0), 0, jnp.maximum(margin, 0))
    shifted = jax.random.randint(jax.random.fold_in(own, 4), (amount // 2,), 0, 1 << 20) % (margin + 1)
    sizes = sizes.at[source_of].add(-shifted).at[sink].add(shifted)
    members = jnp.searchsorted(jnp.cumsum(sizes), jnp.arange(rows * top), side="right").astype(jnp.int32)
    grid = members.reshape(top, rows).T
    grid = grid[jax.random.permutation(jax.random.fold_in(own, 1), rows)]
    turn = jax.random.randint(jax.random.fold_in(own, 2), (rows, 1), 0, top)
    return jnp.take_along_axis(grid, (jnp.arange(top)[None, :] + turn) % top, axis=1)


def shares(count, total, bound, lean, full):
    portions = [(1 << 20) // math.isqrt(rank ** lean) + 1 for rank in range(1, count + 1)]
    largest = bound if full else min(bound, max(-(-total // count), total * portions[0] // sum(portions)))
    least = 1 if total - largest >= count - 1 else 0
    given, spare = [largest] + [least] * (count - 1), total - largest - least * (count - 1)
    while spare > 0:
        free = [i for i in range(1, count) if given[i] < largest] or [i for i in range(1, count) if given[i] < bound]
        whole, left = sum([portions[i] for i in free]), spare
        for i in free:
            more = min(bound - given[i], max(1, left * portions[i] // whole), spare)
            given[i] = given[i] + more
            spare = spare - more
    return np.array(given)


def gaussian(key, dims, width, most, cuts=(), dtype=jnp.bfloat16):
    factor_of = level_of(key, dims, cuts, -0.22, 0.18) if cuts else 1.0
    values = jax.random.normal(key, dims, jnp.float32) * width * factor_of
    return jnp.minimum(jnp.maximum(values, -most), most).astype(dtype)


def setup_inputs(seed: int = 0) -> dict:
    splits = jax.random.split(jax.random.key(seed), 8)
    arriving = gaussian(splits[0], (N_SECTION, TOKENS, D), 1.0, 6.0, ((0, 8), (1, 32)))
    top_grad = gaussian(splits[1], (TICKS - 1, TOKENS, D), 1.0, 6.0, ((1, 32),))
    expert_ids_keys = jax.random.split(jax.random.fold_in(splits[2], 1), N_SECTION * TICKS * TOKENS // MB_DEV)
    expert_ids_turns = jax.random.permutation(jax.random.fold_in(splits[2], 3), N_SECTION * TICKS * TOKENS // MB_DEV)
    expert_ids = jax.vmap(lambda own, number: assign_block(jax.random.fold_in(splits[2], 2), own, number, MB_DEV, EXPERTS, 2, CAP, 2))(expert_ids_keys, expert_ids_turns).reshape((N_SECTION, TICKS, TOKENS, 2))
    first_share = jnp.clip(0.5 + 0.45 * jax.random.uniform(splits[3], (N_SECTION, TICKS, TOKENS), jnp.float32) ** level_of(splits[3], (N_SECTION, TICKS, TOKENS), ((0, 8), (2, 32)), -0.2, 0.2), 0.5, 0.95)
    out_gap = gaussian(splits[4], (N_SECTION, TICKS, TOKENS, D), 1.0, 6.0, ((0, 8), (2, 32)))
    router_weight = gaussian(splits[5], (N_SECTION, EXPERTS, D), 0.05, 0.75, ((0, 8),), jnp.float32)
    down_weight = gaussian(splits[6], (N_SECTION, EXPERTS * FF, D), D ** -0.5, 0.109375, ((0, 8), (1, 32)))
    return dict(arriving=arriving, top_grad=top_grad, expert_ids=expert_ids, first_share=first_share, out_gap=out_gap, router_weight=router_weight, down_weight=down_weight)


def tick_ref(gradient, expert_ids, first_part, gap, router_rows, down_rows):
    gap_dot = jnp.sum(gradient.astype(jnp.float32) * gap.astype(jnp.float32), 1)
    second = 1.0 - first_part
    logit_grad = first_part * second * gap_dot
    expert_range = jnp.arange(EXPERTS)
    select = (expert_ids[:, 0:1] == expert_range).astype(jnp.float32) - (expert_ids[:, 1:2] == expert_range).astype(jnp.float32)
    router_term = jnp.dot(logit_grad[:, None] * select, router_rows, precision=lax.Precision.HIGHEST)
    departing = (gradient.astype(jnp.float32) + router_term).astype(jnp.bfloat16)
    weights = jnp.stack([first_part, second], 1)
    routed_rows = (weights[:, :, None] * gradient.astype(jnp.float32)[:, None, :]).astype(jnp.bfloat16).reshape(-1, D)
    flat_ids = expert_ids.reshape(-1)
    pieces = []
    for expert in range(EXPERTS):
        chosen = (flat_ids == expert).astype(jnp.int32)
        position = jnp.cumsum(chosen) - chosen
        target = jnp.where(chosen == 1, position, MAXP)
        compact = jnp.zeros((MAXP, D), jnp.bfloat16).at[target].set(routed_rows, mode="drop")
        product = lax.dot_general(compact, down_rows[expert * FF:(expert + 1) * FF], (((1,), (1,)), ((), ())), preferred_element_type=jnp.float32).astype(jnp.bfloat16)
        pieces.append(product.reshape(MAXP, GROUP, HID_DEV).transpose(1, 0, 2))
    hidden = jnp.concatenate(pieces, 0).reshape(N_EP * MAXP, HID_DEV)
    return departing, hidden


def reference(arriving, top_grad, expert_ids, first_share, out_gap, router_weight, down_weight):
    departs = [[None] * TICKS for section in range(N_SECTION)]
    hiddens = [[None] * TICKS for section in range(N_SECTION)]
    for moment in range(TICKS):
        for section in range(N_SECTION):
            if moment == 0:
                gradient = arriving[section]
            elif section == N_SECTION - 1:
                gradient = top_grad[moment - 1]
            else:
                gradient = departs[section + 1][moment - 1]
            result = tick_ref(gradient, expert_ids[section, moment], first_share[section, moment], out_gap[section, moment], router_weight[section], down_weight[section])
            departs[section][moment] = result[0]
            hiddens[section][moment] = result[1]
    departing = jnp.stack([jnp.stack(row) for row in departs])
    hidden_grad = jnp.stack([jnp.stack(row) for row in hiddens])
    return departing, hidden_grad
```

```python
import jax
import jax.numpy as jnp
from jax import lax
from jax.sharding import PartitionSpec as P

TICKS = 2
CAP = 36
XS, YS, CORES = 4, 4, 2


def hop(shard, dy=0, dx=0, dc=0):
    pairs = []
    for y in range(YS):
        for x in range(XS):
            for c in range(CORES):
                to = (((y + dy) % YS) * XS + (x + dx) % XS) * CORES + (c + dc) % CORES
                pairs.append(((y * XS + x) * CORES + c, to))
    return lax.ppermute(shard, "ep", pairs)


def down(shard):
    n = lax.axis_size("section")
    return lax.ppermute(shard, "section", [(i, i - 1) for i in range(1, n)])


def route(gradient, own_ids, first_part, my_y):
    tokens = gradient.shape[0]
    flat_ids = own_ids.reshape(-1)
    experts = jnp.arange(YS)
    chosen = (flat_ids[:, None] == experts).astype(jnp.int32)
    ranks = jnp.sum((jnp.cumsum(chosen, 0) - chosen) * chosen, 1)
    places = (((flat_ids - my_y) % YS) * CAP + ranks).reshape(tokens, 2)
    slots = jnp.arange(YS * CAP)[:, None]
    one = slots == places[None, :, 0]
    two = slots == places[None, :, 1]
    weight = jnp.sum(jnp.where(one, first_part, 0.0) + jnp.where(two, 1.0 - first_part, 0.0), 1)
    placing = (one | two).astype(jnp.bfloat16)
    rows = jnp.dot(placing, gradient, preferred_element_type=jnp.float32)
    return (rows * weight[:, None]).astype(jnp.bfloat16)


def router(gradient, own_ids, first_part, gap, router_rows):
    gap_dot = jnp.sum(gradient.astype(jnp.float32) * gap.astype(jnp.float32), 1)
    logit_grad = first_part * (1.0 - first_part) * gap_dot
    first = own_ids[:, 0:1]
    second = own_ids[:, 1:2]
    term = jnp.zeros(gradient.shape, jnp.float32)
    for e in range(YS):
        sign = (first == e).astype(jnp.float32) - (second == e).astype(jnp.float32)
        term = term + (logit_grad[:, None] * sign) * router_rows[e][None, :]
    return (gradient.astype(jnp.float32) + term).astype(jnp.bfloat16)


def exchange(rows):
    part = [rows[j * CAP : (j + 1) * CAP] for j in range(YS)]
    block = jnp.concatenate([part[0]] + [hop(part[j], dy=j) for j in range(1, YS)], 0)
    half = 2 * CAP
    left = hop(block, dx=1)
    right = hop(block, dx=-1)
    far_a = hop(left[:half], dx=1)
    far_b = hop(right[half:], dx=-1)
    got = {0: [block], 1: [left], 3: [right], 2: [far_a, far_b]}
    out = {}
    for d, pieces in got.items():
        out[d, 0] = pieces
        out[d, 1] = [hop(p, dc=1) for p in pieces]
    return out


def experts_product(got, all_ids, down_rows, my_y, my_x, my_c):
    ep_count = lax.axis_size("ep")
    from_each = jnp.sum((all_ids.reshape(ep_count, -1) == my_y).astype(jnp.int32), 1)
    offsets = jnp.cumsum(from_each) - from_each
    prods, targets = [], []
    slot = jnp.arange(CAP)
    for (dx, dc), pieces in got.items():
        for piece in pieces:
            prods.append(
                lax.dot_general(piece, down_rows, (((1,), (1,)), ((), ())), preferred_element_type=jnp.float32).astype(
                    jnp.bfloat16
                )
            )
        for dy in range(YS):
            source = (((my_y - dy) % YS) * XS + (my_x - dx) % XS) * CORES + (my_c - dc) % CORES
            count = from_each[source]
            targets.append(jnp.where(slot < count, offsets[source] + slot, -1))
    targets = jnp.concatenate(targets)
    products = jnp.concatenate(prods, 0)
    total = ep_count * CAP
    placing = (jnp.arange(total)[:, None] == targets[None, :]).astype(jnp.bfloat16)
    return jnp.dot(placing, products, preferred_element_type=jnp.float32).astype(jnp.bfloat16)


def local(arriving, top_grad, expert_ids, first_share, out_gap, router_weight, down_weight):
    section_now = lax.axis_index("section")
    section_count = lax.axis_size("section")
    me = lax.axis_index("ep")
    my_y, my_x, my_c = me // (XS * CORES), (me // CORES) % XS, me % CORES
    gradient = arriving[0]
    tokens = gradient.shape[0]
    departs = []
    hiddens = []
    for moment in range(TICKS):
        if moment > 0:
            gradient = jnp.where(section_now == section_count - 1, top_grad[moment - 1], down(departs[-1]))
        all_ids = expert_ids[0, moment]
        own_ids = lax.dynamic_slice_in_dim(all_ids, me * tokens, tokens, 0)
        first_part = first_share[0, moment]
        rows = route(gradient, own_ids, first_part, my_y)
        departs.append(router(gradient, own_ids, first_part, out_gap[0, moment], router_weight[0]))
        got = exchange(rows)
        hiddens.append(experts_product(got, all_ids, down_weight[0], my_y, my_x, my_c))
    return (jnp.stack(departs)[None], jnp.stack(hiddens)[None])


def solution(mesh):
    placed = (
        P("section", "ep", None),
        P(None, "ep", None),
        P("section", None, None, None),
        P("section", None, "ep"),
        P("section", None, "ep", None),
        P("section", None, None),
        P("section", "ep", None),
    )
    return jax.shard_map(
        local,
        mesh=mesh,
        in_specs=placed,
        out_specs=(P("section", None, "ep", None), P("section", None, "ep", None)),
        check_vma=False,
    )
```

```python
import functools

import jax
import jax.numpy as jnp
import numpy as np
from jax import lax
from jax.experimental import pallas as pl
from jax.experimental.pallas import tpu as pltpu
from jax.sharding import PartitionSpec as P

TICKS = 2
CAP = 36
XS, YS, CORES = 4, 4, 2
EP = XS * YS * CORES
TOKENS = 64
D = 3072
HID = 1024
MAXP = EP * CAP
BLOCK = YS * CAP
HEAD = 80
DYS = (0, 1, 3, 2)
DXS = (0, 1, 3, 2)
WIDE = 256
VMEM = pl.BlockSpec(memory_space=pltpu.VMEM)
ANY = pl.BlockSpec(memory_space=pl.ANY)
NT = (((1,), (1,)), ((), ()))


def hop(shard, dy=0, dx=0, dc=0):
    pairs = []
    for y in range(YS):
        for x in range(XS):
            for c in range(CORES):
                to = (((y + dy) % YS) * XS + (x + dx) % XS) * CORES + (c + dc) % CORES
                pairs.append(((y * XS + x) * CORES + c, to))
    return lax.ppermute(shard, "ep", pairs)


def down(shard):
    n = lax.axis_size("section")
    return lax.ppermute(shard, "section", [(i, i - 1) for i in range(1, n)])


def own_ids_of(ids_ref, moment, me):
    both = ids_ref[moment, :, pl.ds(pl.multiple_of((me // 2) * 128, 128), 128)].astype(jnp.float32)
    return jnp.where(me % 2 == 0, both[:, :TOKENS], both[:, TOKENS:])


def gradient_of(refs):
    if len(refs) == 1:
        return refs[0][...]
    top, moved = refs
    last = lax.axis_index("section") == lax.axis_size("section") - 1
    return jnp.where(last, top[...], moved[...])


def route_kernel(moment, ids_ref, share_ref, *refs):
    grads, outs = refs[:-YS], refs[-YS:]
    me = lax.axis_index("ep")
    my_y = (me // (XS * CORES)).astype(jnp.float32)
    own = own_ids_of(ids_ref, moment, me)
    first, second = own[0:1], own[1:2]
    experts = lax.broadcasted_iota(jnp.int32, (8, TOKENS), 0).astype(jnp.float32)
    is_first, is_second = experts == first, experts == second
    chosen = (is_first | is_second).astype(jnp.float32).astype(jnp.bfloat16)
    before = lax.broadcasted_iota(jnp.int32, (TOKENS, TOKENS), 0) < lax.broadcasted_iota(
        jnp.int32, (TOKENS, TOKENS), 1
    )
    ranks = jnp.dot(chosen, before.astype(jnp.float32).astype(jnp.bfloat16), preferred_element_type=jnp.float32)

    def place(expert, mask):
        relative = expert - my_y
        relative = jnp.where(relative < 0, relative + YS, relative)
        return relative * CAP + jnp.sum(jnp.where(mask, ranks, 0.0), 0, keepdims=True)

    place_1, place_2 = place(first, is_first), place(second, is_second)
    share = share_ref[moment : moment + 1, :]
    gradient = gradient_of(grads)
    slots = lax.broadcasted_iota(jnp.int32, (CAP, TOKENS), 0).astype(jnp.float32)
    for j in range(YS):
        one, two = slots + j * CAP == place_1, slots + j * CAP == place_2
        weight = jnp.sum(jnp.where(one, share, 0.0) + jnp.where(two, 1.0 - share, 0.0), 1, keepdims=True)
        placing = (one | two).astype(jnp.float32).astype(jnp.bfloat16)
        rows = jnp.dot(placing, gradient, preferred_element_type=jnp.float32)
        outs[j][...] = (rows * weight).astype(jnp.bfloat16)


def route(moment, ids, share, grads):
    return pl.pallas_call(
        functools.partial(route_kernel, moment),
        out_shape=[jax.ShapeDtypeStruct((CAP, D), jnp.bfloat16)] * YS,
        in_specs=[VMEM] * (2 + len(grads)),
        out_specs=[VMEM] * YS,
        compiler_params=pltpu.CompilerParams(vmem_limit_bytes=16 << 20),
        cost_estimate=pl.CostEstimate(flops=2 * BLOCK * TOKENS * D, bytes_accessed=2 * 208 * D, transcendentals=0),
        name="route",
    )(ids, share, *grads)


def router_kernel(moment, count, ids_ref, share_ref, router_ref, gap_ref, *refs):
    grads, outs = refs[:count], refs[-2:]
    me = lax.axis_index("ep")
    own = own_ids_of(ids_ref, moment, me)
    eye = lax.broadcasted_iota(jnp.int32, (TOKENS, TOKENS), 0) == lax.broadcasted_iota(
        jnp.int32, (TOKENS, TOKENS), 1
    )

    def upright(row):
        return jnp.sum(jnp.where(eye, row, 0.0), 1, keepdims=True)

    first, second = upright(own[0:1]), upright(own[1:2])
    share = upright(share_ref[moment : moment + 1, :])
    gradient = gradient_of(grads).astype(jnp.float32)
    gap_dot = jnp.sum(gradient * gap_ref[0].astype(jnp.float32), 1, keepdims=True)
    logit_grad = share * (1.0 - share) * gap_dot
    term = jnp.zeros((TOKENS, D), jnp.float32)
    for e in range(YS):
        sign = jnp.where(first == e, 1.0, 0.0) - jnp.where(second == e, 1.0, 0.0)
        term = term + (logit_grad * sign) * router_ref[e : e + 1, :]
    departing = (gradient + term).astype(jnp.bfloat16)
    outs[0][0] = departing
    outs[1][...] = departing


def router(moment, ids, share, router_rows, gap, grads, departs):
    more = [] if departs is None else [departs]
    return pl.pallas_call(
        functools.partial(router_kernel, moment, len(grads)),
        grid=(1,),
        out_shape=[
            jax.ShapeDtypeStruct((TICKS, TOKENS, D), jnp.bfloat16),
            jax.ShapeDtypeStruct((TOKENS, D), jnp.bfloat16),
        ],
        in_specs=[VMEM] * 3
        + [pl.BlockSpec((1, TOKENS, D), lambda i: (moment, 0, 0))]
        + [VMEM] * len(grads)
        + [ANY] * len(more),
        out_specs=[pl.BlockSpec((1, TOKENS, D), lambda i: (moment, 0, 0)), VMEM],
        input_output_aliases={4 + len(grads): 0} if more else {},
        compiler_params=pltpu.CompilerParams(vmem_limit_bytes=16 << 20),
        cost_estimate=pl.CostEstimate(flops=12 * TOKENS * D, bytes_accessed=2 * 256 * D, transcendentals=0),
        name="router",
    )(ids, share, router_rows, gap, *grads, *more)


def experts_kernel(moment, sizes, earlier, ids_ref, table_ref, *refs):
    count = len(sizes)
    pieces, down_ref = refs[:count], refs[count]
    out_ref, rows_ref, placing_ref, sems = refs[-4:]
    total = sum(sizes)

    @pl.when(pl.program_id(0) == 0)
    def _():
        copies, begin = [], 0
        for i, size in enumerate(sizes):
            copies.append(pltpu.make_async_copy(pieces[i], rows_ref.at[pl.ds(begin, size)], sems.at[i]))
            copies[-1].start()
            begin += size
        me = lax.axis_index("ep")
        my_y, my_x, my_c = me // (XS * CORES), (me // CORES) % XS, me % CORES
        named = (ids_ref[moment] == my_y).astype(jnp.float32)
        named = jnp.broadcast_to(named[0:1] + named[1:2], (8, EP * TOKENS)).astype(jnp.bfloat16)
        owner = lax.broadcasted_iota(jnp.int32, (EP, EP * TOKENS), 1) // TOKENS
        owned = owner == lax.broadcasted_iota(jnp.int32, (EP, EP * TOKENS), 0)
        counts = lax.dot_general(
            named, owned.astype(jnp.float32).astype(jnp.bfloat16), NT, preferred_element_type=jnp.float32
        ).astype(jnp.bfloat16)
        table = table_ref[...]
        source = (
            ((my_y - table[0:1]) & (YS - 1)) * (XS * CORES)
            + ((my_x - table[1:2]) & (XS - 1)) * CORES
            + ((my_c - table[2:3]) & (CORES - 1))
        )
        slot = table[3:4].astype(jnp.float32)
        device = lax.broadcasted_iota(jnp.int32, (EP, total), 0)
        ahead = (device < source).astype(jnp.float32).astype(jnp.bfloat16)
        itself = (device == source).astype(jnp.float32).astype(jnp.bfloat16)
        offset = jnp.dot(counts, ahead, preferred_element_type=jnp.float32)[0:1]
        amount = jnp.dot(counts, itself, preferred_element_type=jnp.float32)[0:1]
        target = jnp.where(slot < amount, offset + slot, -1.0).astype(jnp.int32)
        step = 128

        @pl.loop(0, MAXP // step)
        def _(k):
            at = pl.multiple_of(k * step, step)
            here = lax.broadcasted_iota(jnp.int32, (step, total), 0) + at
            placing_ref[pl.ds(at, step), :] = (here == target).astype(jnp.float32).astype(jnp.bfloat16)

        for copy in copies:
            copy.wait()

    product = lax.dot_general(rows_ref[...], down_ref[...], NT, preferred_element_type=jnp.float32)
    placed = jnp.dot(placing_ref[...], product.astype(jnp.bfloat16), preferred_element_type=jnp.float32)
    if earlier:
        placed = placed + refs[count + 1][0].astype(jnp.float32)
    out_ref[0] = placed.astype(jnp.bfloat16)


def experts(moment, ids, groups, down_rows, hidden, earlier):
    pieces, columns = [], []
    for dx, dc, parts in groups:
        pieces += parts
        for dy in DYS:
            columns += [(dy, dx, dc, slot) for slot in range(CAP)]
    table = np.zeros((8, len(columns)), np.int32)
    table[:4] = np.array(columns, np.int32).T
    total = len(columns)
    sizes = tuple(p.shape[0] for p in pieces)
    block = pl.BlockSpec((1, MAXP, WIDE), lambda n: (moment, 0, n))
    more = [] if hidden is None else [hidden]
    return pl.pallas_call(
        functools.partial(experts_kernel, moment, sizes, earlier),
        grid=(HID // WIDE,),
        out_shape=jax.ShapeDtypeStruct((TICKS, MAXP, HID), jnp.bfloat16),
        in_specs=[VMEM, VMEM]
        + [ANY] * len(pieces)
        + [pl.BlockSpec((WIDE, D), lambda n: (n, 0))]
        + ([block if earlier else ANY] if more else []),
        out_specs=block,
        scratch_shapes=[
            pltpu.VMEM((total, D), jnp.bfloat16),
            pltpu.VMEM((MAXP, total), jnp.bfloat16),
            pltpu.SemaphoreType.DMA((len(pieces),)),
        ],
        input_output_aliases={3 + len(pieces): 0} if more else {},
        compiler_params=pltpu.CompilerParams(vmem_limit_bytes=32 << 20),
        cost_estimate=pl.CostEstimate(
            flops=2 * total * HID * (D + MAXP),
            bytes_accessed=2 * (total * D + HID * D + MAXP * HID * (2 if earlier else 1)),
            transcendentals=0,
        ),
        name="experts",
    )(ids, jnp.asarray(table), *pieces, down_rows, *more)


def exchange(parts):
    r1, r3, r2 = hop(parts[1], dy=1), hop(parts[3], dy=3), hop(parts[2], dy=2)
    split = HEAD - 2 * CAP
    head = jnp.concatenate([parts[0], r1, r3[:split]], 0)
    tail = jnp.concatenate([r3[split:], r2], 0)
    got = {0: (head, tail)}
    got[1] = (hop(head, dx=1), hop(tail, dx=1))
    got[3] = (hop(head, dx=3), hop(tail, dx=3))
    got[2] = (hop(got[1][0], dx=1), hop(got[3][1], dx=3))
    out = {}
    for dx in DXS:
        out[dx, 0] = got[dx]
        out[dx, 1] = tuple(hop(p, dc=1) for p in got[dx])
    return out


def local(arriving, top_grad, expert_ids, first_share, out_gap, router_weight, down_weight):
    ids = jnp.swapaxes(expert_ids[0], 1, 2)
    share, gap, router_rows, down_rows = first_share[0], out_gap[0], router_weight[0], down_weight[0]
    grads = [arriving[0]]
    departs = hidden = None
    for moment in range(TICKS):
        parts = route(moment, ids, share, grads)
        departs, departing = router(moment, ids, share, router_rows, gap, grads, departs)
        got = exchange(parts)
        early = [(dx, dc, got[dx, dc]) for dx in DXS[:3] for dc in range(CORES)]
        late = [(dx, dc, got[dx, dc]) for dx in DXS[3:] for dc in range(CORES)]
        hidden = experts(moment, ids, early, down_rows, hidden, False)
        hidden = experts(moment, ids, late, down_rows, hidden, True)
        if moment + 1 < TICKS:
            grads = [top_grad[moment], down(departing)]
    return departs[None], hidden[None]


def solution(mesh):
    placed = (
        P("section", "ep", None),
        P(None, "ep", None),
        P("section", None, None, None),
        P("section", None, "ep"),
        P("section", None, "ep", None),
        P("section", None, None),
        P("section", "ep", None),
    )
    return jax.shard_map(
        local,
        mesh=mesh,
        in_specs=placed,
        out_specs=(P("section", None, "ep", None), P("section", None, "ep", None)),
        check_vma=False,
    )
```

```python
import functools

import jax
import jax.numpy as jnp
import numpy as np
from jax import lax
from jax.experimental import pallas as pl
from jax.experimental.pallas import tpu as pltpu
from jax.sharding import PartitionSpec as P

TICKS = 2
CAP = 36
XS, YS, CORES = 4, 4, 2
EP = XS * YS * CORES
TOKENS = 64
D = 3072
HID = 1024
MAXP = EP * CAP
BLOCK = YS * CAP
HEAD = 80
DYS = (0, 1, 3, 2)
GROUP = CORES * BLOCK
STEP = 128
PLACED = 384
VMEM = pl.BlockSpec(memory_space=pltpu.VMEM)
ANY = pl.BlockSpec(memory_space=pl.ANY)
CHEAP = pl.CostEstimate(flops=1024, bytes_accessed=1024, transcendentals=0)
NT = (((1,), (1,)), ((), ()))


def hop(shard, dy=0, dx=0, dc=0):
    pairs = []
    for y in range(YS):
        for x in range(XS):
            for c in range(CORES):
                to = (((y + dy) % YS) * XS + (x + dx) % XS) * CORES + (c + dc) % CORES
                pairs.append(((y * XS + x) * CORES + c, to))
    return lax.ppermute(shard, "ep", pairs)


def down(shard):
    n = lax.axis_size("section")
    return lax.ppermute(shard, "section", [(i, i - 1) for i in range(1, n)])


def own_ids_of(ids_ref, moment, me):
    both = ids_ref[moment, :, pl.ds(pl.multiple_of((me // 2) * 128, 128), 128)].astype(jnp.float32)
    return jnp.where(me % 2 == 0, both[:, :TOKENS], both[:, TOKENS:])


def gradient_of(refs):
    if len(refs) == 1:
        return refs[0][...]
    top, moved = refs
    last = lax.axis_index("section") == lax.axis_size("section") - 1
    return jnp.where(last, top[...], moved[...])


def route_kernel(moment, ids_ref, share_ref, *refs):
    grads, outs = refs[:-YS], refs[-YS:]
    me = lax.axis_index("ep")
    my_y = (me // (XS * CORES)).astype(jnp.float32)
    own = own_ids_of(ids_ref, moment, me)
    first, second = own[0:1], own[1:2]
    experts = lax.broadcasted_iota(jnp.int32, (8, TOKENS), 0).astype(jnp.float32)
    is_first, is_second = experts == first, experts == second
    chosen = (is_first | is_second).astype(jnp.float32).astype(jnp.bfloat16)
    before = lax.broadcasted_iota(jnp.int32, (TOKENS, TOKENS), 0) < lax.broadcasted_iota(
        jnp.int32, (TOKENS, TOKENS), 1
    )
    ranks = jnp.dot(chosen, before.astype(jnp.float32).astype(jnp.bfloat16), preferred_element_type=jnp.float32)

    def place(expert, mask):
        relative = expert - my_y
        relative = jnp.where(relative < 0, relative + YS, relative)
        return relative * CAP + jnp.sum(jnp.where(mask, ranks, 0.0), 0, keepdims=True)

    place_1, place_2 = place(first, is_first), place(second, is_second)
    share = share_ref[moment : moment + 1, :]
    gradient = gradient_of(grads)
    slots = lax.broadcasted_iota(jnp.int32, (CAP, TOKENS), 0).astype(jnp.float32)
    for j in range(YS):
        one, two = slots + j * CAP == place_1, slots + j * CAP == place_2
        weight = jnp.sum(jnp.where(one, share, 0.0) + jnp.where(two, 1.0 - share, 0.0), 1, keepdims=True)
        placing = (one | two).astype(jnp.float32).astype(jnp.bfloat16)
        rows = jnp.dot(placing, gradient, preferred_element_type=jnp.float32)
        outs[j][...] = (rows * weight).astype(jnp.bfloat16)


def whole(array):
    rank = len(array.shape)
    return pl.BlockSpec(array.shape, lambda i: (0,) * rank)


def route(moment, ids, share, grads):
    return pl.pallas_call(
        functools.partial(route_kernel, moment),
        grid=(1,),
        out_shape=[jax.ShapeDtypeStruct((CAP, D), jnp.bfloat16)] * YS,
        in_specs=[whole(a) for a in (ids, share, *grads)],
        out_specs=[pl.BlockSpec((CAP, D), lambda i: (0, 0))] * YS,
        compiler_params=pltpu.CompilerParams(vmem_limit_bytes=16 << 20),
        cost_estimate=CHEAP,
        name="route",
    )(ids, share, *grads)


def router_kernel(moment, count, ids_ref, share_ref, router_ref, gap_ref, *refs):
    grads, outs = refs[:count], refs[-2:]
    me = lax.axis_index("ep")
    own = own_ids_of(ids_ref, moment, me)
    eye = lax.broadcasted_iota(jnp.int32, (TOKENS, TOKENS), 0) == lax.broadcasted_iota(
        jnp.int32, (TOKENS, TOKENS), 1
    )

    def upright(row):
        return jnp.sum(jnp.where(eye, row, 0.0), 1, keepdims=True)

    first, second = upright(own[0:1]), upright(own[1:2])
    share = upright(share_ref[moment : moment + 1, :])
    gradient = gradient_of(grads).astype(jnp.float32)
    gap_dot = jnp.sum(gradient * gap_ref[0].astype(jnp.float32), 1, keepdims=True)
    logit_grad = share * (1.0 - share) * gap_dot
    term = jnp.zeros((TOKENS, D), jnp.float32)
    for e in range(YS):
        sign = jnp.where(first == e, 1.0, 0.0) - jnp.where(second == e, 1.0, 0.0)
        term = term + (logit_grad * sign) * router_ref[e : e + 1, :]
    departing = (gradient + term).astype(jnp.bfloat16)
    outs[0][0] = departing
    outs[1][...] = departing


def router(moment, ids, share, router_rows, gap, grads, departs):
    more = [] if departs is None else [departs]
    return pl.pallas_call(
        functools.partial(router_kernel, moment, len(grads)),
        grid=(1,),
        out_shape=[
            jax.ShapeDtypeStruct((TICKS, TOKENS, D), jnp.bfloat16),
            jax.ShapeDtypeStruct((TOKENS, D), jnp.bfloat16),
        ],
        in_specs=[whole(a) for a in (ids, share, router_rows)]
        + [pl.BlockSpec((1, TOKENS, D), lambda i: (moment, 0, 0))]
        + [whole(a) for a in grads]
        + [ANY] * len(more),
        out_specs=[
            pl.BlockSpec((1, TOKENS, D), lambda i: (moment, 0, 0)),
            pl.BlockSpec((TOKENS, D), lambda i: (0, 0)),
        ],
        input_output_aliases={4 + len(grads): 0} if more else {},
        compiler_params=pltpu.CompilerParams(vmem_limit_bytes=16 << 20),
        cost_estimate=CHEAP,
        name="router",
    )(ids, share, router_rows, gap, *grads, *more)


def load_rows(pieces, rows_ref, sems):
    copies, begin = [], 0
    for i, piece in enumerate(pieces):
        size = piece.shape[0]
        copies.append((begin, pltpu.make_async_copy(piece, rows_ref.at[pl.ds(begin, size)], sems.at[i])))
        copies[i][1].start()
        begin += size
    return copies


def multiply(copies, rows_ref, down_ref, product_ref, base):
    for begin in range(0, rows_ref.shape[0], GROUP):
        for at, copy in copies:
            if begin <= at < begin + GROUP:
                copy.wait()
        product = lax.dot_general(
            rows_ref[pl.ds(begin, GROUP), :], down_ref[...], NT, preferred_element_type=jnp.float32
        )
        product_ref[pl.ds(base + begin, GROUP), :] = product.astype(jnp.bfloat16)


def near_kernel(count, down_ref, *refs):
    product_ref, rows_ref, sems = refs[count:]
    multiply(load_rows(refs[:count], rows_ref, sems), rows_ref, down_ref, product_ref, 0)


def near_product(pieces, down_rows):
    total = sum(p.shape[0] for p in pieces)
    return pl.pallas_call(
        functools.partial(near_kernel, len(pieces)),
        out_shape=jax.ShapeDtypeStruct((total, HID), jnp.bfloat16),
        in_specs=[VMEM] + [ANY] * len(pieces),
        out_specs=VMEM,
        scratch_shapes=[pltpu.VMEM((total, D), jnp.bfloat16), pltpu.SemaphoreType.DMA((len(pieces),))],
        compiler_params=pltpu.CompilerParams(vmem_limit_bytes=24 << 20),
        cost_estimate=CHEAP,
        name="near_product",
    )(down_rows, *pieces)


def place_kernel(moment, count, ids_ref, table_ref, down_ref, *refs):
    pieces, near_ref = refs[:count], refs[count]
    out_ref, rows_ref, placing_ref, product_ref, placed_ref, sems = refs[-6:]
    copies = load_rows(pieces, rows_ref, sems)
    base = MAXP - rows_ref.shape[0]
    back = pltpu.make_async_copy(near_ref, product_ref.at[pl.ds(0, base)], sems.at[count])
    back.start()
    me = lax.axis_index("ep")
    my_y, my_x, my_c = me // (XS * CORES), (me // CORES) % XS, me % CORES
    named = (ids_ref[moment] == my_y).astype(jnp.float32)
    named = jnp.broadcast_to(named[0:1] + named[1:2], (8, EP * TOKENS)).astype(jnp.bfloat16)
    owner = lax.broadcasted_iota(jnp.int32, (EP, EP * TOKENS), 1) // TOKENS
    owned = owner == lax.broadcasted_iota(jnp.int32, (EP, EP * TOKENS), 0)
    counts = lax.dot_general(
        named, owned.astype(jnp.float32).astype(jnp.bfloat16), NT, preferred_element_type=jnp.float32
    ).astype(jnp.bfloat16)
    table = table_ref[...]
    source = (
        ((my_y - table[0:1]) & (YS - 1)) * (XS * CORES)
        + ((my_x - table[1:2]) & (XS - 1)) * CORES
        + ((my_c - table[2:3]) & (CORES - 1))
    )
    slot = table[3:4].astype(jnp.float32)
    device = lax.broadcasted_iota(jnp.int32, (EP, MAXP), 0)
    ahead = (device < source).astype(jnp.float32).astype(jnp.bfloat16)
    itself = (device == source).astype(jnp.float32).astype(jnp.bfloat16)
    offset = jnp.dot(counts, ahead, preferred_element_type=jnp.float32)[0:1]
    amount = jnp.dot(counts, itself, preferred_element_type=jnp.float32)[0:1]
    target = jnp.where(slot < amount, offset + slot, -1.0).astype(jnp.int32)

    @pl.loop(0, MAXP // STEP)
    def _(k):
        at = pl.multiple_of(k * STEP, STEP)
        here = lax.broadcasted_iota(jnp.int32, (STEP, MAXP), 0) + at
        placing_ref[pl.ds(at, STEP), :] = (here == target).astype(jnp.float32).astype(jnp.bfloat16)

    multiply(copies, rows_ref, down_ref, product_ref, base)
    back.wait()
    stores = []
    for k in range(MAXP // PLACED):
        part = pl.ds(k * PLACED, PLACED)
        placed = jnp.dot(placing_ref[part, :], product_ref[...], preferred_element_type=jnp.float32)
        placed_ref[part, :] = placed.astype(jnp.bfloat16)
        stores.append(
            pltpu.make_async_copy(placed_ref.at[part], out_ref.at[moment, part], sems.at[count + 1 + k])
        )
        stores[k].start()
    for store in stores:
        store.wait()


def place(moment, ids, pieces, near, order, down_rows, hidden):
    columns = [(dy, dx, dc, slot) for dx, dc in order for dy in DYS for slot in range(CAP)]
    table = np.zeros((8, MAXP), np.int32)
    table[:4] = np.array(columns, np.int32).T
    more = [] if hidden is None else [hidden]
    return pl.pallas_call(
        functools.partial(place_kernel, moment, len(pieces)),
        out_shape=jax.ShapeDtypeStruct((TICKS, MAXP, HID), jnp.bfloat16),
        in_specs=[VMEM] * 3 + [ANY] * (len(pieces) + 1 + len(more)),
        out_specs=ANY,
        scratch_shapes=[
            pltpu.VMEM((sum(p.shape[0] for p in pieces), D), jnp.bfloat16),
            pltpu.VMEM((MAXP, MAXP), jnp.bfloat16),
            pltpu.VMEM((MAXP, HID), jnp.bfloat16),
            pltpu.VMEM((MAXP, HID), jnp.bfloat16),
            pltpu.SemaphoreType.DMA((len(pieces) + 1 + MAXP // PLACED,)),
        ],
        input_output_aliases={4 + len(pieces): 0} if more else {},
        compiler_params=pltpu.CompilerParams(vmem_limit_bytes=24 << 20),
        cost_estimate=CHEAP,
        name="place",
    )(ids, jnp.asarray(table), down_rows, *pieces, near, *more)


def spread(parts):
    return {j: hop(parts[j], dy=j) for j in (1, 3, 2)}


def joined(own, came):
    return jnp.concatenate([own, came[1], came[3], came[2]], 0)


def beside(block):
    return {dx: hop(block, dx=dx) for dx in (1, 3)}


def opposite(near):
    return hop(near[1][:HEAD], dx=1), hop(near[3][HEAD:], dx=3)


def swapped(tree):
    return jax.tree.map(lambda p: hop(p, dc=1), tree)


NEAR = ((0, 0), (0, 1), (1, 0), (1, 1), (3, 0), (3, 1))
FAR = ((2, 0), (2, 1))


def local(arriving, top_grad, expert_ids, first_share, out_gap, router_weight, down_weight):
    tie = lax.optimization_barrier
    ids = jnp.swapaxes(expert_ids[0], 1, 2)
    share, gap, router_rows, down_rows = first_share[0], out_gap[0], router_weight[0], down_weight[0]

    parts0 = route(0, ids, share, [arriving[0]])
    parts0, gradient = tie((parts0, arriving[0]))
    departs, departing = router(0, ids, share, router_rows, gap, [gradient], None)
    own0, came0, moved = tie((parts0[0], spread(parts0), down(departing)))

    block0 = joined(own0, came0)
    near0 = beside(block0)
    grads = [top_grad[0], moved]
    parts1 = route(1, ids, share, grads)
    own1, came1, block0, near0, grads = tie((parts1[0], spread(parts1), block0, near0, grads))

    block1 = joined(own1, came1)
    far0 = opposite(near0)
    near1 = beside(block1)
    mate0, mates0 = swapped(block0), swapped(near0)
    pieces = [block0, mate0, near0[1], mates0[1], near0[3], mates0[3]]
    product0 = near_product(pieces, down_rows)
    departs, _ = router(1, ids, share, router_rows, gap, grads, departs)
    far0, block1, near1, product0, departs = tie((far0, block1, near1, product0, departs))

    far1 = opposite(near1)
    mate = swapped(far0)
    mate1, mates1 = swapped(block1), swapped(near1)
    hidden = place(0, ids, [*far0, *mate], product0, NEAR + FAR, down_rows, None)
    far1, near1, block1, mate1, mates1, hidden = tie((far1, near1, block1, mate1, mates1, hidden))

    mate = swapped(far1)
    pieces = [block1, mate1, near1[1], mates1[1], near1[3], mates1[3]]
    product1 = near_product(pieces, down_rows)
    hidden = place(1, ids, [*far1, *mate], product1, NEAR + FAR, down_rows, hidden)
    return departs[None], hidden[None]


def solution(mesh):
    placed = (
        P("section", "ep", None),
        P(None, "ep", None),
        P("section", None, None, None),
        P("section", None, "ep"),
        P("section", None, "ep", None),
        P("section", None, None),
        P("section", "ep", None),
    )
    return jax.shard_map(
        local,
        mesh=mesh,
        in_specs=placed,
        out_specs=(P("section", None, "ep", None), P("section", None, "ep", None)),
        check_vma=False,
    )
```

```python
import functools

import jax
import jax.numpy as jnp
import numpy as np
from jax import lax
from jax.experimental import pallas as pl
from jax.experimental.pallas import tpu as pltpu
from jax.sharding import PartitionSpec as P

TICKS = 2
CAP = 36
XS, YS, CORES = 4, 4, 2
EP = XS * YS * CORES
TOKENS = 64
D = 3072
HID = 1024
MAXP = EP * CAP
BLOCK = YS * CAP
HEAD = 80
DYS = (0, 1, 3, 2)
GROUP = CORES * BLOCK
STEP = 128
PLACED = 384
ORDER = ((0, 0), (1, 0), (3, 0), (0, 1), (1, 1), (3, 1), (2, 0), (2, 1))
VMEM = pl.BlockSpec(memory_space=pltpu.VMEM)
ANY = pl.BlockSpec(memory_space=pl.ANY)
HBM = pl.BlockSpec(memory_space=pltpu.HBM)
CHEAP = pl.CostEstimate(flops=1024, bytes_accessed=1024, transcendentals=0)
SOME = pl.CostEstimate(flops=1200 << 20, bytes_accessed=1024, transcendentals=0)
NT = (((1,), (1,)), ((), ()))


def hop(shard, dy=0, dx=0, dc=0):
    pairs = []
    for y in range(YS):
        for x in range(XS):
            for c in range(CORES):
                to = (((y + dy) % YS) * XS + (x + dx) % XS) * CORES + (c + dc) % CORES
                pairs.append(((y * XS + x) * CORES + c, to))
    return lax.ppermute(shard, "ep", pairs)


def down(shard):
    n = lax.axis_size("section")
    return lax.ppermute(shard, "section", [(i, i - 1) for i in range(1, n)])


def front_kernel(moment, count, ids_hbm, share_hbm, router_hbm, gap_hbm, *refs):
    grads, outs = refs[:count], refs[-14:-8]
    ids_ref, share_ref, router_ref, gap_ref, grads_ref, parts_ref, departing_ref, sems = refs[-8:]
    pairs = [(ids_hbm.at[moment], ids_ref), (share_hbm, share_ref)]
    pairs += [(grads[i], grads_ref.at[i]) for i in range(count)]
    pairs += [(gap_hbm.at[moment], gap_ref), (router_hbm, router_ref)]
    loads = [pltpu.make_async_copy(source, to, sems.at[i]) for i, (source, to) in enumerate(pairs)]
    for load in loads:
        load.start()
    for load in loads[: 2 + count]:
        load.wait()
    me = lax.axis_index("ep")
    both = ids_ref[:, pl.ds(pl.multiple_of((me // 2) * 128, 128), 128)].astype(jnp.float32)
    own = jnp.where(me % 2 == 0, both[:, :TOKENS], both[:, TOKENS:])
    first, second = own[0:1], own[1:2]
    share = share_ref[moment : moment + 1, :]
    gradient = grads_ref[0]
    if count == 2:
        last = lax.axis_index("section") == lax.axis_size("section") - 1
        gradient = jnp.where(last, gradient, grads_ref[1])

    my_y = (me // (XS * CORES)).astype(jnp.float32)
    experts = lax.broadcasted_iota(jnp.int32, (8, TOKENS), 0).astype(jnp.float32)
    is_first, is_second = experts == first, experts == second
    chosen = (is_first | is_second).astype(jnp.float32).astype(jnp.bfloat16)
    rows = lax.broadcasted_iota(jnp.int32, (TOKENS, TOKENS), 0)
    columns = lax.broadcasted_iota(jnp.int32, (TOKENS, TOKENS), 1)
    before = (rows < columns).astype(jnp.float32).astype(jnp.bfloat16)
    ranks = jnp.dot(chosen, before, preferred_element_type=jnp.float32)

    def placed(expert, mask):
        relative = expert - my_y
        relative = jnp.where(relative < 0, relative + YS, relative)
        return relative * CAP + jnp.sum(jnp.where(mask, ranks, 0.0), 0, keepdims=True)

    place_1, place_2 = placed(first, is_first), placed(second, is_second)
    slots = lax.broadcasted_iota(jnp.int32, (CAP, TOKENS), 0).astype(jnp.float32)
    stores = []
    for j in range(YS):
        one, two = slots + j * CAP == place_1, slots + j * CAP == place_2
        weight = jnp.sum(jnp.where(one, share, 0.0) + jnp.where(two, 1.0 - share, 0.0), 1, keepdims=True)
        placing = (one | two).astype(jnp.float32).astype(jnp.bfloat16)
        gathered = jnp.dot(placing, gradient, preferred_element_type=jnp.float32)
        parts_ref[j] = (gathered * weight).astype(jnp.bfloat16)
        stores.append(pltpu.make_async_copy(parts_ref.at[j], outs[j], sems.at[4 + count + j]))
        stores[j].start()

    def upright(row):
        return jnp.sum(jnp.where(rows == columns, row, 0.0), 1, keepdims=True)

    for load in loads[2 + count :]:
        load.wait()
    first, second, share = upright(first), upright(second), upright(share)
    gradient = gradient.astype(jnp.float32)
    gap_dot = jnp.sum(gradient * gap_ref[...].astype(jnp.float32), 1, keepdims=True)
    logit_grad = share * (1.0 - share) * gap_dot
    term = jnp.zeros((TOKENS, D), jnp.float32)
    for e in range(YS):
        sign = jnp.where(first == e, 1.0, 0.0) - jnp.where(second == e, 1.0, 0.0)
        term = term + (logit_grad * sign) * router_ref[e : e + 1, :]
    departing_ref[...] = (gradient + term).astype(jnp.bfloat16)
    for to in (outs[YS].at[moment], outs[YS + 1]):
        stores.append(pltpu.make_async_copy(departing_ref, to, sems.at[4 + count + len(stores)]))
        stores[-1].start()
    for store in stores:
        store.wait()


def front(moment, ids, share, router_rows, gap, grads, departs):
    more = [] if departs is None else [departs]
    count = len(grads)
    return pl.pallas_call(
        functools.partial(front_kernel, moment, count),
        out_shape=[jax.ShapeDtypeStruct((CAP, D), jnp.bfloat16)] * YS
        + [
            jax.ShapeDtypeStruct((TICKS, TOKENS, D), jnp.bfloat16),
            jax.ShapeDtypeStruct((TOKENS, D), jnp.bfloat16),
        ],
        in_specs=[HBM] * (4 + count + len(more)),
        out_specs=[HBM] * (YS + 2),
        scratch_shapes=[
            pltpu.VMEM((2, EP * TOKENS), jnp.int32),
            pltpu.VMEM((TICKS, TOKENS), jnp.float32),
            pltpu.VMEM((YS, D), jnp.float32),
            pltpu.VMEM((TOKENS, D), jnp.bfloat16),
            pltpu.VMEM((count, TOKENS, D), jnp.bfloat16),
            pltpu.VMEM((YS, CAP, D), jnp.bfloat16),
            pltpu.VMEM((TOKENS, D), jnp.bfloat16),
            pltpu.SemaphoreType.DMA((4 + count + YS + 2,)),
        ],
        input_output_aliases={4 + count: YS} if more else {},
        compiler_params=pltpu.CompilerParams(vmem_limit_bytes=(16 if more else 60) << 20),
        cost_estimate=CHEAP,
        name="front",
    )(ids, share, router_rows, gap, *grads, *more)


def load_rows(pieces, rows_ref, sems):
    copies, begin = [], 0
    for i, piece in enumerate(pieces):
        size = piece.shape[0]
        copies.append((begin, pltpu.make_async_copy(piece, rows_ref.at[pl.ds(begin, size)], sems.at[i])))
        copies[i][1].start()
        begin += size
    return copies


def multiply(copies, rows_ref, down_ref, product_ref, base):
    for begin in range(0, rows_ref.shape[0], GROUP):
        for at, copy in copies:
            if begin <= at < begin + GROUP:
                copy.wait()
        product = lax.dot_general(
            rows_ref[pl.ds(begin, GROUP), :], down_ref[...], NT, preferred_element_type=jnp.float32
        )
        product_ref[pl.ds(base + begin, GROUP), :] = product.astype(jnp.bfloat16)


def near_kernel(count, down_ref, *refs):
    product_ref, rows_ref, sems = refs[count:]
    multiply(load_rows(refs[:count], rows_ref, sems), rows_ref, down_ref, product_ref, 0)


def near_product(pieces, down_rows):
    total = sum(p.shape[0] for p in pieces)
    return pl.pallas_call(
        functools.partial(near_kernel, len(pieces)),
        out_shape=jax.ShapeDtypeStruct((total, HID), jnp.bfloat16),
        in_specs=[VMEM] + [ANY] * len(pieces),
        out_specs=VMEM,
        scratch_shapes=[pltpu.VMEM((total, D), jnp.bfloat16), pltpu.SemaphoreType.DMA((len(pieces),))],
        compiler_params=pltpu.CompilerParams(vmem_limit_bytes=24 << 20),
        cost_estimate=CHEAP,
        name="near_product",
    )(down_rows, *pieces)


def plan_kernel(ids_ref, table_ref, *outs):
    me = lax.axis_index("ep")
    my_y, my_x, my_c = me // (XS * CORES), (me // CORES) % XS, me % CORES
    table = table_ref[...]
    source = (
        ((my_y - table[0:1]) & (YS - 1)) * (XS * CORES)
        + ((my_x - table[1:2]) & (XS - 1)) * CORES
        + ((my_c - table[2:3]) & (CORES - 1))
    )
    slot = table[3:4].astype(jnp.float32)
    device = lax.broadcasted_iota(jnp.int32, (EP, MAXP), 0)
    ahead = (device < source).astype(jnp.float32).astype(jnp.bfloat16)
    itself = (device == source).astype(jnp.float32).astype(jnp.bfloat16)
    owner = lax.broadcasted_iota(jnp.int32, (EP, EP * TOKENS), 1) // TOKENS
    owned = (owner == lax.broadcasted_iota(jnp.int32, (EP, EP * TOKENS), 0)).astype(jnp.float32).astype(jnp.bfloat16)
    for moment in range(TICKS):
        named = (ids_ref[moment] == my_y).astype(jnp.float32)
        named = jnp.broadcast_to(named[0:1] + named[1:2], (8, EP * TOKENS)).astype(jnp.bfloat16)
        counts = lax.dot_general(named, owned, NT, preferred_element_type=jnp.float32).astype(jnp.bfloat16)
        offset = jnp.dot(counts, ahead, preferred_element_type=jnp.float32)[0:1]
        amount = jnp.dot(counts, itself, preferred_element_type=jnp.float32)[0:1]
        target = jnp.where(slot < amount, offset + slot, -1.0).astype(jnp.int32)

        @pl.loop(0, MAXP // STEP)
        def _(k):
            at = pl.multiple_of(k * STEP, STEP)
            here = lax.broadcasted_iota(jnp.int32, (STEP, MAXP), 0) + at
            outs[moment][pl.ds(at, STEP), :] = (here == target).astype(jnp.float32).astype(jnp.bfloat16)


def plan(ids):
    columns = [(dy, dx, dc, slot) for dx, dc in ORDER for dy in DYS for slot in range(CAP)]
    table = np.zeros((8, MAXP), np.int32)
    table[:4] = np.array(columns, np.int32).T
    return pl.pallas_call(
        plan_kernel,
        out_shape=[jax.ShapeDtypeStruct((MAXP, MAXP), jnp.bfloat16)] * TICKS,
        in_specs=[VMEM] * 2,
        out_specs=[VMEM] * TICKS,
        compiler_params=pltpu.CompilerParams(vmem_limit_bytes=16 << 20),
        cost_estimate=CHEAP,
        name="plan",
    )(ids, jnp.asarray(table))


def place_kernel(moment, count, placing_ref, down_ref, *refs):
    pieces, near_ref = refs[:count], refs[count]
    out_ref, rows_ref, product_ref, placed_ref, sems = refs[-5:]
    copies = load_rows(pieces, rows_ref, sems)
    base = MAXP - rows_ref.shape[0]
    back = pltpu.make_async_copy(near_ref, product_ref.at[pl.ds(0, base)], sems.at[count])
    back.start()
    multiply(copies, rows_ref, down_ref, product_ref, base)
    back.wait()
    stores = []
    for k in range(MAXP // PLACED):
        part = pl.ds(k * PLACED, PLACED)
        placed = jnp.dot(placing_ref[part, :], product_ref[...], preferred_element_type=jnp.float32)
        placed_ref[part, :] = placed.astype(jnp.bfloat16)
        stores.append(
            pltpu.make_async_copy(placed_ref.at[part], out_ref.at[moment, part], sems.at[count + 1 + k])
        )
        stores[k].start()
    for store in stores:
        store.wait()


def place(moment, placing, pieces, near, down_rows, hidden):
    more = [] if hidden is None else [hidden]
    return pl.pallas_call(
        functools.partial(place_kernel, moment, len(pieces)),
        out_shape=jax.ShapeDtypeStruct((TICKS, MAXP, HID), jnp.bfloat16),
        in_specs=[VMEM] * 2 + [ANY] * (len(pieces) + 1 + len(more)),
        out_specs=ANY,
        scratch_shapes=[
            pltpu.VMEM((sum(p.shape[0] for p in pieces), D), jnp.bfloat16),
            pltpu.VMEM((MAXP, HID), jnp.bfloat16),
            pltpu.VMEM((MAXP, HID), jnp.bfloat16),
            pltpu.SemaphoreType.DMA((len(pieces) + 1 + MAXP // PLACED,)),
        ],
        input_output_aliases={3 + len(pieces): 0} if more else {},
        compiler_params=pltpu.CompilerParams(vmem_limit_bytes=24 << 20),
        cost_estimate=SOME,
        name="place",
    )(placing, down_rows, *pieces, near, *more)


def spread(parts):
    return {j: hop(parts[j], dy=j) for j in (1, 3, 2)}


def joined(own, came):
    return jnp.concatenate([own, came[1], came[3], came[2]], 0)


def beside(block):
    return {dx: hop(block, dx=dx) for dx in (1, 3)}


def opposite(near):
    return hop(near[1][:HEAD], dx=1), hop(near[3][HEAD:], dx=3)


def swapped(tree):
    return jax.tree.map(lambda p: hop(p, dc=1), tree)


def local(arriving, top_grad, expert_ids, first_share, out_gap, router_weight, down_weight):
    tie = lax.optimization_barrier
    ids = jnp.swapaxes(expert_ids[0], 1, 2)
    share, gap, router_rows, down_rows = first_share[0], out_gap[0], router_weight[0], down_weight[0]

    *parts0, departs, departing = front(0, ids, share, router_rows, gap, [arriving[0]], None)
    placing = plan(ids)
    own0, came0, moved, placing = tie((parts0[0], spread(parts0), down(departing), placing))

    block0 = joined(own0, came0)
    near0 = beside(block0)
    *parts1, departs, _ = front(1, ids, share, router_rows, gap, [top_grad[0], moved], departs)
    own1, came1, block0, near0 = tie((parts1[0], spread(parts1), block0, near0))

    block1 = joined(own1, came1)
    far0 = opposite(near0)
    near1 = beside(block1)
    pieces = [block0, near0[1], near0[3]]
    product0 = near_product([*pieces, swapped(jnp.concatenate(pieces))], down_rows)
    hidden = place(0, placing[0], [*far0, *swapped(far0)], product0, down_rows, None)
    block1, near1, hidden = tie((block1, near1, hidden))

    far1 = opposite(near1)
    pieces = [block1, near1[1], near1[3]]
    product1 = near_product([*pieces, swapped(jnp.concatenate(pieces))], down_rows)
    far1, product1 = tie((far1, product1))

    hidden = place(1, placing[1], [*far1, *swapped(far1)], product1, down_rows, hidden)
    return departs[None], hidden[None]


def solution(mesh):
    placed = (
        P("section", "ep", None),
        P(None, "ep", None),
        P("section", None, None, None),
        P("section", None, "ep"),
        P("section", None, "ep", None),
        P("section", None, None),
        P("section", "ep", None),
    )
    return jax.shard_map(
        local,
        mesh=mesh,
        in_specs=placed,
        out_specs=(P("section", None, "ep", None), P("section", None, "ep", None)),
        check_vma=False,
    )
```

```python
import functools

import jax
import jax.numpy as jnp
import numpy as np
from jax import lax
from jax.experimental import pallas as pl
from jax.experimental.pallas import tpu as pltpu
from jax.sharding import PartitionSpec as P

TICKS = 2
CAP = 36
XS, YS, CORES = 4, 4, 2
EP = XS * YS * CORES
TOKENS = 64
D = 3072
HID = 1024
MAXP = EP * CAP
BLOCK = YS * CAP
HEAD = 80
DYS = (0, 1, 3, 2)
GROUP = CORES * BLOCK
NEAR = 3 * GROUP
OWN = 32
STEP = 128
PLACED = 384
ORDER = ((0, 0), (1, 0), (3, 0), (0, 1), (1, 1), (3, 1), (2, 0), (2, 1))
VMEM = pl.BlockSpec(memory_space=pltpu.VMEM)
ANY = pl.BlockSpec(memory_space=pl.ANY)
HBM = pl.BlockSpec(memory_space=pltpu.HBM)
CHEAP = pl.CostEstimate(flops=1024, bytes_accessed=1024, transcendentals=0)
SOME = pl.CostEstimate(flops=1200 << 20, bytes_accessed=1024, transcendentals=0)
NT = (((1,), (1,)), ((), ()))


def hop(shard, dy=0, dx=0, dc=0):
    pairs = []
    for y in range(YS):
        for x in range(XS):
            for c in range(CORES):
                to = (((y + dy) % YS) * XS + (x + (dx, -dx)[c]) % XS) * CORES + (c + dc) % CORES
                pairs.append(((y * XS + x) * CORES + c, to))
    return lax.ppermute(shard, "ep", pairs)


def down(shard):
    n = lax.axis_size("section")
    return lax.ppermute(shard, "section", [(i, i - 1) for i in range(1, n)])


def front_kernel(moment, count, ids_hbm, share_hbm, router_hbm, gap_hbm, *refs):
    grads, outs = refs[:count], refs[-15:-8]
    ids_ref, share_ref, router_ref, gap_ref, grads_ref, parts_ref, departing_ref, sems = refs[-8:]
    pairs = [(ids_hbm.at[moment], ids_ref), (share_hbm, share_ref)]
    pairs += [(grads[i], grads_ref.at[i]) for i in range(count)]
    pairs += [(gap_hbm.at[moment], gap_ref), (router_hbm, router_ref)]
    loads = [pltpu.make_async_copy(source, to, sems.at[i]) for i, (source, to) in enumerate(pairs)]
    for load in loads:
        load.start()
    for load in loads[: 2 + count]:
        load.wait()
    me = lax.axis_index("ep")
    both = ids_ref[:, pl.ds(pl.multiple_of((me // 2) * 128, 128), 128)].astype(jnp.float32)
    own = jnp.where(me % 2 == 0, both[:, :TOKENS], both[:, TOKENS:])
    first, second = own[0:1], own[1:2]
    share = share_ref[moment : moment + 1, :]
    gradient = grads_ref[0]
    if count == 2:
        last = lax.axis_index("section") == lax.axis_size("section") - 1
        gradient = jnp.where(last, gradient, grads_ref[1])

    my_y = (me // (XS * CORES)).astype(jnp.float32)
    experts = lax.broadcasted_iota(jnp.int32, (8, TOKENS), 0).astype(jnp.float32)
    is_first, is_second = experts == first, experts == second
    chosen = (is_first | is_second).astype(jnp.float32).astype(jnp.bfloat16)
    rows = lax.broadcasted_iota(jnp.int32, (TOKENS, TOKENS), 0)
    columns = lax.broadcasted_iota(jnp.int32, (TOKENS, TOKENS), 1)
    before = (rows < columns).astype(jnp.float32).astype(jnp.bfloat16)
    ranks = jnp.dot(chosen, before, preferred_element_type=jnp.float32)

    def placed(expert, mask):
        relative = expert - my_y
        relative = jnp.where(relative < 0, relative + YS, relative)
        return relative * CAP + jnp.sum(jnp.where(mask, ranks, 0.0), 0, keepdims=True)

    place_1, place_2 = placed(first, is_first), placed(second, is_second)
    slots = lax.broadcasted_iota(jnp.int32, (CAP, TOKENS), 0).astype(jnp.float32)
    stores = []
    for j in range(YS):
        one, two = slots + j * CAP == place_1, slots + j * CAP == place_2
        weight = jnp.sum(jnp.where(one, share, 0.0) + jnp.where(two, 1.0 - share, 0.0), 1, keepdims=True)
        placing = (one | two).astype(jnp.float32).astype(jnp.bfloat16)
        gathered = jnp.dot(placing, gradient, preferred_element_type=jnp.float32)
        parts_ref[j] = (gathered * weight).astype(jnp.bfloat16)
        stores.append(pltpu.make_async_copy(parts_ref.at[j], outs[j], sems.at[4 + count + j]))
        stores[j].start()
    stores.append(pltpu.make_async_copy(parts_ref.at[0, pl.ds(0, OWN)], outs[YS], sems.at[4 + count + YS]))
    stores[YS].start()

    def upright(row):
        return jnp.sum(jnp.where(rows == columns, row, 0.0), 1, keepdims=True)

    for load in loads[2 + count :]:
        load.wait()
    first, second, share = upright(first), upright(second), upright(share)
    gradient = gradient.astype(jnp.float32)
    gap_dot = jnp.sum(gradient * gap_ref[...].astype(jnp.float32), 1, keepdims=True)
    logit_grad = share * (1.0 - share) * gap_dot
    term = jnp.zeros((TOKENS, D), jnp.float32)
    for e in range(YS):
        sign = jnp.where(first == e, 1.0, 0.0) - jnp.where(second == e, 1.0, 0.0)
        term = term + (logit_grad * sign) * router_ref[e : e + 1, :]
    departing_ref[...] = (gradient + term).astype(jnp.bfloat16)
    for to in (outs[YS + 1].at[moment], outs[YS + 2]):
        stores.append(pltpu.make_async_copy(departing_ref, to, sems.at[4 + count + len(stores)]))
        stores[-1].start()
    for store in stores:
        store.wait()


def front(moment, ids, share, router_rows, gap, grads, departs):
    more = [] if departs is None else [departs]
    count = len(grads)
    return pl.pallas_call(
        functools.partial(front_kernel, moment, count),
        out_shape=[jax.ShapeDtypeStruct((CAP, D), jnp.bfloat16)] * YS
        + [
            jax.ShapeDtypeStruct((OWN, D), jnp.bfloat16),
            jax.ShapeDtypeStruct((TICKS, TOKENS, D), jnp.bfloat16),
            jax.ShapeDtypeStruct((TOKENS, D), jnp.bfloat16),
        ],
        in_specs=[HBM] * (4 + count + len(more)),
        out_specs=[HBM] * (YS + 3),
        scratch_shapes=[
            pltpu.VMEM((2, EP * TOKENS), jnp.int32),
            pltpu.VMEM((TICKS, TOKENS), jnp.float32),
            pltpu.VMEM((YS, D), jnp.float32),
            pltpu.VMEM((TOKENS, D), jnp.bfloat16),
            pltpu.VMEM((count, TOKENS, D), jnp.bfloat16),
            pltpu.VMEM((YS, CAP, D), jnp.bfloat16),
            pltpu.VMEM((TOKENS, D), jnp.bfloat16),
            pltpu.SemaphoreType.DMA((4 + count + YS + 3,)),
        ],
        input_output_aliases={4 + count: YS + 1} if more else {},
        compiler_params=pltpu.CompilerParams(vmem_limit_bytes=60 << 20),
        cost_estimate=CHEAP,
        name="front",
    )(ids, share, router_rows, gap, *grads, *more)


def multiply(pieces, rows_ref, down_ref, product_ref):
    begin = 0
    for piece in pieces:
        rows_ref[pl.ds(begin, piece.shape[0]), :] = piece[...]
        begin += piece.shape[0]
    for at in range(0, begin, GROUP):
        part = pl.ds(at, GROUP)
        product = lax.dot_general(rows_ref[part, :], down_ref[...], NT, preferred_element_type=jnp.float32)
        product_ref[part, :] = product.astype(jnp.bfloat16)


def plan_kernel(ids_ref, table_ref, *outs):
    me = lax.axis_index("ep")
    my_y, my_x, my_c = me // (XS * CORES), (me // CORES) % XS, me % CORES
    table = table_ref[...]
    source_c = (my_c - table[2:3]) & (CORES - 1)
    source_x = jnp.where(source_c == 0, my_x - table[1:2], my_x + table[1:2]) & (XS - 1)
    source = ((my_y - table[0:1]) & (YS - 1)) * (XS * CORES) + source_x * CORES + source_c
    slot = table[3:4].astype(jnp.float32)
    device = lax.broadcasted_iota(jnp.int32, (EP, MAXP), 0)
    ahead = (device < source).astype(jnp.float32).astype(jnp.bfloat16)
    itself = (device == source).astype(jnp.float32).astype(jnp.bfloat16)
    owner = lax.broadcasted_iota(jnp.int32, (EP, EP * TOKENS), 1) // TOKENS
    owned = (owner == lax.broadcasted_iota(jnp.int32, (EP, EP * TOKENS), 0)).astype(jnp.float32).astype(jnp.bfloat16)
    for moment in range(TICKS):
        named = (ids_ref[moment] == my_y).astype(jnp.float32)
        named = jnp.broadcast_to(named[0:1] + named[1:2], (8, EP * TOKENS)).astype(jnp.bfloat16)
        counts = lax.dot_general(named, owned, NT, preferred_element_type=jnp.float32).astype(jnp.bfloat16)
        offset = jnp.dot(counts, ahead, preferred_element_type=jnp.float32)[0:1]
        amount = jnp.dot(counts, itself, preferred_element_type=jnp.float32)[0:1]
        target = jnp.where(slot < amount, offset + slot, -1.0).astype(jnp.int32)

        for i, part in enumerate((target[:, :NEAR], target[:, NEAR:])):

            @pl.loop(0, MAXP // STEP)
            def _(k, out=outs[2 * moment + i], part=part):
                at = pl.multiple_of(k * STEP, STEP)
                here = lax.broadcasted_iota(jnp.int32, (STEP, part.shape[1]), 0) + at
                out[pl.ds(at, STEP), :] = (here == part).astype(jnp.float32).astype(jnp.bfloat16)


def plan(ids):
    columns = [(dy, dx, dc, slot) for dx, dc in ORDER for dy in DYS for slot in range(CAP)]
    table = np.zeros((8, MAXP), np.int32)
    table[:4] = np.array(columns, np.int32).T
    return pl.pallas_call(
        plan_kernel,
        out_shape=[jax.ShapeDtypeStruct((MAXP, n), jnp.bfloat16) for n in (NEAR, GROUP)] * TICKS,
        in_specs=[VMEM] * 2,
        out_specs=[VMEM] * (2 * TICKS),
        compiler_params=pltpu.CompilerParams(vmem_limit_bytes=16 << 20),
        cost_estimate=CHEAP,
        name="plan",
    )(ids, jnp.asarray(table))


def near_kernel(count, placing_ref, down_ref, *refs):
    out_ref, rows_ref, product_ref = refs[count:]
    multiply(refs[:count], rows_ref, down_ref, product_ref)
    for k in range(MAXP // PLACED):
        part = pl.ds(k * PLACED, PLACED)
        placed = jnp.dot(placing_ref[part, :], product_ref[...], preferred_element_type=jnp.float32)
        out_ref[part, :] = placed.astype(jnp.bfloat16)


def near_product(placing, pieces, down_rows):
    return pl.pallas_call(
        functools.partial(near_kernel, len(pieces)),
        out_shape=jax.ShapeDtypeStruct((MAXP, HID), jnp.bfloat16),
        in_specs=[VMEM] * (2 + len(pieces)),
        out_specs=VMEM,
        scratch_shapes=[
            pltpu.VMEM((NEAR, D), jnp.bfloat16),
            pltpu.VMEM((NEAR, HID), jnp.bfloat16),
        ],
        compiler_params=pltpu.CompilerParams(vmem_limit_bytes=24 << 20),
        cost_estimate=CHEAP,
        name="near_product",
    )(placing, down_rows, *pieces)


def far_kernel(moment, count, placing_ref, down_ref, near_ref, *refs):
    out_ref, rows_ref, product_ref, placed_ref, sems = refs[-5:]
    multiply(refs[:count], rows_ref, down_ref, product_ref)
    stores = []
    for k in range(MAXP // PLACED):
        part = pl.ds(k * PLACED, PLACED)
        placed = jnp.dot(placing_ref[part, :], product_ref[...], preferred_element_type=jnp.float32)
        placed_ref[part, :] = (placed + near_ref[part, :].astype(jnp.float32)).astype(jnp.bfloat16)
        stores.append(pltpu.make_async_copy(placed_ref.at[part], out_ref.at[moment, part], sems.at[k]))
        stores[k].start()
    for store in stores:
        store.wait()


def far_product(moment, placing, pieces, near, down_rows, hidden):
    more = [] if hidden is None else [hidden]
    return pl.pallas_call(
        functools.partial(far_kernel, moment, len(pieces)),
        out_shape=jax.ShapeDtypeStruct((TICKS, MAXP, HID), jnp.bfloat16),
        in_specs=[VMEM] * (3 + len(pieces)) + [ANY] * len(more),
        out_specs=ANY,
        scratch_shapes=[
            pltpu.VMEM((GROUP, D), jnp.bfloat16),
            pltpu.VMEM((GROUP, HID), jnp.bfloat16),
            pltpu.VMEM((MAXP, HID), jnp.bfloat16),
            pltpu.SemaphoreType.DMA((MAXP // PLACED,)),
        ],
        input_output_aliases={3 + len(pieces): 0} if more else {},
        compiler_params=pltpu.CompilerParams(vmem_limit_bytes=24 << 20),
        cost_estimate=SOME,
        name="far_product",
    )(placing, down_rows, near, *pieces, *more)


def spread(parts):
    return {j: hop(parts[j], dy=j) for j in (1, 3, 2)}


def joined(own, came):
    return jnp.concatenate([own, came[1], came[3], came[2]], 0)


def opposite(near):
    lead, *more = near[1]
    lead = jnp.concatenate([lead, more[0][: HEAD - OWN]]) if more else lead[:HEAD]
    return hop(lead, dx=1), hop(near[3][0][HEAD:], dx=3)


def swapped(tree):
    return jax.tree.map(lambda p: hop(p, dc=1), tree)


def local(arriving, top_grad, expert_ids, first_share, out_gap, router_weight, down_weight):
    tie = lax.optimization_barrier
    ids = jnp.swapaxes(expert_ids[0], 1, 2)
    share, gap, router_rows, down_rows = first_share[0], out_gap[0], router_weight[0], down_weight[0]

    *parts0, head0, departs, departing = front(0, ids, share, router_rows, gap, [arriving[0]], None)
    grads = [top_grad[0], down(departing)]
    *parts1, _, departs, _ = front(1, ids, share, router_rows, gap, grads, departs)
    first0 = hop(head0, dx=1)
    own0, came0, first0, parts1, departs = tie((parts0[0], spread(parts0), first0, parts1, departs))

    block0 = joined(own0, came0)
    near0 = {1: [first0, hop(block0[OWN:], dx=1)], 3: [hop(block0, dx=3)]}
    placing = plan(ids)
    own1, came1, block0, near0, placing = tie((parts1[0], spread(parts1), block0, near0, placing))

    block1 = joined(own1, came1)
    far0 = opposite(near0)
    near1 = {dx: [hop(block1, dx=dx)] for dx in (1, 3)}
    pieces = [block0, *near0[1], *near0[3]]
    product0 = near_product(placing[0], [*pieces, swapped(jnp.concatenate(pieces))], down_rows)
    hidden = far_product(0, placing[1], [*far0, *swapped(far0)], product0, down_rows, None)
    block1, near1, hidden = tie((block1, near1, hidden))

    far1 = opposite(near1)
    pieces = [block1, *near1[1], *near1[3]]
    product1 = near_product(placing[2], [*pieces, swapped(jnp.concatenate(pieces))], down_rows)
    far1, product1 = tie((far1, product1))

    hidden = far_product(1, placing[3], [*far1, *swapped(far1)], product1, down_rows, hidden)
    return departs[None], hidden[None]


def solution(mesh):
    placed = (
        P("section", "ep", None),
        P(None, "ep", None),
        P("section", None, None, None),
        P("section", None, "ep"),
        P("section", None, "ep", None),
        P("section", None, None),
        P("section", "ep", None),
    )
    return jax.shard_map(
        local,
        mesh=mesh,
        in_specs=placed,
        out_specs=(P("section", None, "ep", None), P("section", None, "ep", None)),
        check_vma=False,
    )
```

```python
import functools

import jax
import jax.numpy as jnp
import numpy as np
from jax import lax
from jax.experimental import pallas as pl
from jax.experimental.pallas import tpu as pltpu
from jax.sharding import PartitionSpec as P

TICKS = 2
CAP = 36
XS, YS, CORES = 4, 4, 2
EP = XS * YS * CORES
TOKENS = 64
D = 3072
HID = 1024
MAXP = EP * CAP
BLOCK = YS * CAP
HEAD = 80
DYS = (0, 1, 3, 2)
GROUP = CORES * BLOCK
NEAR = 3 * GROUP
OWN = 32
STEP = 128
PLACED = 384
ORDER = ((0, 0), (1, 0), (3, 0), (0, 1), (1, 1), (3, 1), (2, 0), (2, 1))
VMEM = pl.BlockSpec(memory_space=pltpu.VMEM)
ANY = pl.BlockSpec(memory_space=pl.ANY)
HBM = pl.BlockSpec(memory_space=pltpu.HBM)
CHEAP = pl.CostEstimate(flops=1024, bytes_accessed=1024, transcendentals=0)
SOME = pl.CostEstimate(flops=1200 << 20, bytes_accessed=1024, transcendentals=0)
NT = (((1,), (1,)), ((), ()))


def hop(shard, dy=0, dx=0, dc=0):
    pairs = []
    for y in range(YS):
        for x in range(XS):
            for c in range(CORES):
                to = (((y + dy) % YS) * XS + (x + (dx, -dx)[c]) % XS) * CORES + (c + dc) % CORES
                pairs.append(((y * XS + x) * CORES + c, to))
    return lax.ppermute(shard, "ep", pairs)


def down(shard):
    n = lax.axis_size("section")
    return lax.ppermute(shard, "section", [(i, i - 1) for i in range(1, n)])


def front_kernel(moment, count, ids_hbm, share_hbm, router_hbm, gap_hbm, *refs):
    grads, outs = refs[:count], refs[-15:-8]
    ids_ref, share_ref, router_ref, gap_ref, grads_ref, parts_ref, departing_ref, sems = refs[-8:]
    pairs = [(ids_hbm.at[moment], ids_ref), (share_hbm, share_ref)]
    pairs += [(grads[i], grads_ref.at[i]) for i in range(count)]
    pairs += [(gap_hbm.at[moment], gap_ref), (router_hbm, router_ref)]
    loads = [pltpu.make_async_copy(source, to, sems.at[i]) for i, (source, to) in enumerate(pairs)]
    for load in loads:
        load.start()
    for load in loads[: 2 + count]:
        load.wait()
    me = lax.axis_index("ep")
    both = ids_ref[:, pl.ds(pl.multiple_of((me // 2) * 128, 128), 128)].astype(jnp.float32)
    own = jnp.where(me % 2 == 0, both[:, :TOKENS], both[:, TOKENS:])
    first, second = own[0:1], own[1:2]
    share = share_ref[moment : moment + 1, :]
    gradient = grads_ref[0]
    if count == 2:
        last = lax.axis_index("section") == lax.axis_size("section") - 1
        gradient = jnp.where(last, gradient, grads_ref[1])

    my_y = (me // (XS * CORES)).astype(jnp.float32)
    experts = lax.broadcasted_iota(jnp.int32, (8, TOKENS), 0).astype(jnp.float32)
    is_first, is_second = experts == first, experts == second
    chosen = (is_first | is_second).astype(jnp.float32).astype(jnp.bfloat16)
    rows = lax.broadcasted_iota(jnp.int32, (TOKENS, TOKENS), 0)
    columns = lax.broadcasted_iota(jnp.int32, (TOKENS, TOKENS), 1)
    before = (rows < columns).astype(jnp.float32).astype(jnp.bfloat16)
    ranks = jnp.dot(chosen, before, preferred_element_type=jnp.float32)

    def placed(expert, mask):
        relative = expert - my_y
        relative = jnp.where(relative < 0, relative + YS, relative)
        return relative * CAP + jnp.sum(jnp.where(mask, ranks, 0.0), 0, keepdims=True)

    place_1, place_2 = placed(first, is_first), placed(second, is_second)
    slots = lax.broadcasted_iota(jnp.int32, (CAP, TOKENS), 0).astype(jnp.float32)
    stores = []
    for j in range(YS):
        one, two = slots + j * CAP == place_1, slots + j * CAP == place_2
        weight = jnp.sum(jnp.where(one, share, 0.0) + jnp.where(two, 1.0 - share, 0.0), 1, keepdims=True)
        placing = (one | two).astype(jnp.float32).astype(jnp.bfloat16)
        gathered = jnp.dot(placing, gradient, preferred_element_type=jnp.float32)
        parts_ref[j] = (gathered * weight).astype(jnp.bfloat16)
        stores.append(pltpu.make_async_copy(parts_ref.at[j], outs[j], sems.at[4 + count + j]))
        stores[j].start()
    stores.append(pltpu.make_async_copy(parts_ref.at[0, pl.ds(0, OWN)], outs[YS], sems.at[4 + count + YS]))
    stores[YS].start()

    def upright(row):
        return jnp.sum(jnp.where(rows == columns, row, 0.0), 1, keepdims=True)

    for load in loads[2 + count :]:
        load.wait()
    first, second, share = upright(first), upright(second), upright(share)
    gradient = gradient.astype(jnp.float32)
    gap_dot = jnp.sum(gradient * gap_ref[...].astype(jnp.float32), 1, keepdims=True)
    logit_grad = share * (1.0 - share) * gap_dot
    term = jnp.zeros((TOKENS, D), jnp.float32)
    for e in range(YS):
        sign = jnp.where(first == e, 1.0, 0.0) - jnp.where(second == e, 1.0, 0.0)
        term = term + (logit_grad * sign) * router_ref[e : e + 1, :]
    departing_ref[...] = (gradient + term).astype(jnp.bfloat16)
    for to in (outs[YS + 1].at[moment], outs[YS + 2]):
        stores.append(pltpu.make_async_copy(departing_ref, to, sems.at[4 + count + len(stores)]))
        stores[-1].start()
    for store in stores:
        store.wait()


def front(moment, ids, share, router_rows, gap, grads, departs):
    more = [] if departs is None else [departs]
    count = len(grads)
    return pl.pallas_call(
        functools.partial(front_kernel, moment, count),
        out_shape=[jax.ShapeDtypeStruct((CAP, D), jnp.bfloat16)] * YS
        + [
            jax.ShapeDtypeStruct((OWN, D), jnp.bfloat16),
            jax.ShapeDtypeStruct((TICKS, TOKENS, D), jnp.bfloat16),
            jax.ShapeDtypeStruct((TOKENS, D), jnp.bfloat16),
        ],
        in_specs=[HBM] * (4 + count + len(more)),
        out_specs=[HBM] * (YS + 3),
        scratch_shapes=[
            pltpu.VMEM((2, EP * TOKENS), jnp.int32),
            pltpu.VMEM((TICKS, TOKENS), jnp.float32),
            pltpu.VMEM((YS, D), jnp.float32),
            pltpu.VMEM((TOKENS, D), jnp.bfloat16),
            pltpu.VMEM((count, TOKENS, D), jnp.bfloat16),
            pltpu.VMEM((YS, CAP, D), jnp.bfloat16),
            pltpu.VMEM((TOKENS, D), jnp.bfloat16),
            pltpu.SemaphoreType.DMA((4 + count + YS + 3,)),
        ],
        input_output_aliases={4 + count: YS + 1} if more else {},
        compiler_params=pltpu.CompilerParams(vmem_limit_bytes=60 << 20),
        cost_estimate=CHEAP,
        name="front",
    )(ids, share, router_rows, gap, *grads, *more)


def multiply(pieces, rows_ref, down_ref, product_ref):
    begin = 0
    for piece in pieces:
        rows_ref[pl.ds(begin, piece.shape[0]), :] = piece[...]
        begin += piece.shape[0]

    def group(at):
        part = pl.ds(at, GROUP)
        product = lax.dot_general(rows_ref[part, :], down_ref[...], NT, preferred_element_type=jnp.float32)
        product_ref[part, :] = product.astype(jnp.bfloat16)

    if begin == GROUP:
        group(0)
    else:

        @pl.loop(0, begin // GROUP)
        def _(k):
            group(pl.multiple_of(k * GROUP, GROUP))


def plan_kernel(ids_ref, table_ref, *outs):
    me = lax.axis_index("ep")
    my_y, my_x, my_c = me // (XS * CORES), (me // CORES) % XS, me % CORES
    table = table_ref[...]
    source_c = (my_c - table[2:3]) & (CORES - 1)
    source_x = jnp.where(source_c == 0, my_x - table[1:2], my_x + table[1:2]) & (XS - 1)
    source = ((my_y - table[0:1]) & (YS - 1)) * (XS * CORES) + source_x * CORES + source_c
    slot = table[3:4].astype(jnp.float32)
    device = lax.broadcasted_iota(jnp.int32, (EP, MAXP), 0)
    ahead = (device < source).astype(jnp.float32).astype(jnp.bfloat16)
    itself = (device == source).astype(jnp.float32).astype(jnp.bfloat16)
    owner = lax.broadcasted_iota(jnp.int32, (EP, EP * TOKENS), 1) // TOKENS
    owned = (owner == lax.broadcasted_iota(jnp.int32, (EP, EP * TOKENS), 0)).astype(jnp.float32).astype(jnp.bfloat16)
    for moment in range(TICKS):
        named = (ids_ref[moment] == my_y).astype(jnp.float32)
        named = jnp.broadcast_to(named[0:1] + named[1:2], (8, EP * TOKENS)).astype(jnp.bfloat16)
        counts = lax.dot_general(named, owned, NT, preferred_element_type=jnp.float32).astype(jnp.bfloat16)
        offset = jnp.dot(counts, ahead, preferred_element_type=jnp.float32)[0:1]
        amount = jnp.dot(counts, itself, preferred_element_type=jnp.float32)[0:1]
        target = jnp.where(slot < amount, offset + slot, -1.0).astype(jnp.int32)

        for i, part in enumerate((target[:, :NEAR], target[:, NEAR:])):

            @pl.loop(0, MAXP // STEP)
            def _(k, out=outs[2 * moment + i], part=part):
                at = pl.multiple_of(k * STEP, STEP)
                here = lax.broadcasted_iota(jnp.int32, (STEP, part.shape[1]), 0) + at
                out[pl.ds(at, STEP), :] = (here == part).astype(jnp.float32).astype(jnp.bfloat16)


def plan(ids):
    columns = [(dy, dx, dc, slot) for dx, dc in ORDER for dy in DYS for slot in range(CAP)]
    table = np.zeros((8, MAXP), np.int32)
    table[:4] = np.array(columns, np.int32).T
    return pl.pallas_call(
        plan_kernel,
        out_shape=[jax.ShapeDtypeStruct((MAXP, n), jnp.bfloat16) for n in (NEAR, GROUP)] * TICKS,
        in_specs=[VMEM] * 2,
        out_specs=[VMEM] * (2 * TICKS),
        compiler_params=pltpu.CompilerParams(vmem_limit_bytes=16 << 20),
        cost_estimate=CHEAP,
        name="plan",
    )(ids, jnp.asarray(table))


def near_kernel(count, placing_ref, down_ref, *refs):
    out_ref, rows_ref, product_ref = refs[count:]
    multiply(refs[:count], rows_ref, down_ref, product_ref)

    @pl.loop(0, MAXP // PLACED)
    def _(k):
        part = pl.ds(pl.multiple_of(k * PLACED, PLACED), PLACED)
        placed = jnp.dot(placing_ref[part, :], product_ref[...], preferred_element_type=jnp.float32)
        out_ref[part, :] = placed.astype(jnp.bfloat16)


def near_product(placing, pieces, down_rows):
    return pl.pallas_call(
        functools.partial(near_kernel, len(pieces)),
        out_shape=jax.ShapeDtypeStruct((MAXP, HID), jnp.bfloat16),
        in_specs=[VMEM] * (2 + len(pieces)),
        out_specs=VMEM,
        scratch_shapes=[
            pltpu.VMEM((NEAR, D), jnp.bfloat16),
            pltpu.VMEM((NEAR, HID), jnp.bfloat16),
        ],
        compiler_params=pltpu.CompilerParams(vmem_limit_bytes=24 << 20),
        cost_estimate=CHEAP,
        name="near_product",
    )(placing, down_rows, *pieces)


def far_kernel(moment, count, placing_ref, down_ref, near_ref, *refs):
    out_ref, rows_ref, product_ref, placed_ref, sems = refs[-5:]
    multiply(refs[:count], rows_ref, down_ref, product_ref)
    stores = []
    for k in range(MAXP // PLACED):
        part = pl.ds(k * PLACED, PLACED)
        placed = jnp.dot(placing_ref[part, :], product_ref[...], preferred_element_type=jnp.float32)
        placed_ref[part, :] = (placed + near_ref[part, :].astype(jnp.float32)).astype(jnp.bfloat16)
        stores.append(pltpu.make_async_copy(placed_ref.at[part], out_ref.at[moment, part], sems.at[k]))
        stores[k].start()
    for store in stores:
        store.wait()


def far_product(moment, placing, pieces, near, down_rows, hidden):
    more = [] if hidden is None else [hidden]
    return pl.pallas_call(
        functools.partial(far_kernel, moment, len(pieces)),
        out_shape=jax.ShapeDtypeStruct((TICKS, MAXP, HID), jnp.bfloat16),
        in_specs=[VMEM] * (3 + len(pieces)) + [ANY] * len(more),
        out_specs=ANY,
        scratch_shapes=[
            pltpu.VMEM((GROUP, D), jnp.bfloat16),
            pltpu.VMEM((GROUP, HID), jnp.bfloat16),
            pltpu.VMEM((MAXP, HID), jnp.bfloat16),
            pltpu.SemaphoreType.DMA((MAXP // PLACED,)),
        ],
        input_output_aliases={3 + len(pieces): 0} if more else {},
        compiler_params=pltpu.CompilerParams(vmem_limit_bytes=24 << 20),
        cost_estimate=SOME,
        name="far_product",
    )(placing, down_rows, near, *pieces, *more)


def spread(parts):
    return {j: hop(parts[j], dy=j) for j in (1, 3, 2)}


def joined(own, came):
    return jnp.concatenate([own, came[1], came[3], came[2]], 0)


def opposite(near):
    lead, *more = near[1]
    lead = jnp.concatenate([lead, more[0][: HEAD - OWN]]) if more else lead[:HEAD]
    return hop(lead, dx=1), hop(near[3][0][HEAD:], dx=3)


def swapped(tree):
    return jax.tree.map(lambda p: hop(p, dc=1), tree)


def local(arriving, top_grad, expert_ids, first_share, out_gap, router_weight, down_weight):
    tie = lax.optimization_barrier
    ids = jnp.swapaxes(expert_ids[0], 1, 2)
    share, gap, router_rows, down_rows = first_share[0], out_gap[0], router_weight[0], down_weight[0]

    *parts0, head0, departs, departing = front(0, ids, share, router_rows, gap, [arriving[0]], None)
    grads = [top_grad[0], down(departing)]
    *parts1, _, departs, _ = front(1, ids, share, router_rows, gap, grads, departs)
    first0 = hop(head0, dx=1)
    own0, came0, first0, parts1, departs = tie((parts0[0], spread(parts0), first0, parts1, departs))

    block0 = joined(own0, came0)
    near0 = {1: [first0, hop(block0[OWN:], dx=1)], 3: [hop(block0, dx=3)]}
    placing = plan(ids)
    own1, came1, block0, near0, placing = tie((parts1[0], spread(parts1), block0, near0, placing))

    block1 = joined(own1, came1)
    far0 = opposite(near0)
    near1 = {dx: [hop(block1, dx=dx)] for dx in (1, 3)}
    pieces = [block0, *near0[1], *near0[3]]
    product0 = near_product(placing[0], [*pieces, swapped(jnp.concatenate(pieces))], down_rows)
    hidden = far_product(0, placing[1], [*far0, *swapped(far0)], product0, down_rows, None)
    block1, near1, hidden = tie((block1, near1, hidden))

    far1 = opposite(near1)
    pieces = [block1, *near1[1], *near1[3]]
    product1 = near_product(placing[2], [*pieces, swapped(jnp.concatenate(pieces))], down_rows)
    far1, product1 = tie((far1, product1))

    hidden = far_product(1, placing[3], [*far1, *swapped(far1)], product1, down_rows, hidden)
    return departs[None], hidden[None]


def solution(mesh):
    placed = (
        P("section", "ep", None),
        P(None, "ep", None),
        P("section", None, None, None),
        P("section", None, "ep"),
        P("section", None, "ep", None),
        P("section", None, None),
        P("section", "ep", None),
    )
    return jax.shard_map(
        local,
        mesh=mesh,
        in_specs=placed,
        out_specs=(P("section", None, "ep", None), P("section", None, "ep", None)),
        check_vma=False,
    )
```

```python
import functools

import jax
import jax.numpy as jnp
import numpy as np
from jax import lax
from jax.experimental import pallas as pl
from jax.experimental.pallas import tpu as pltpu
from jax.sharding import PartitionSpec as P

TICKS = 2
CAP = 36
XS, YS, CORES = 4, 4, 2
EP = XS * YS * CORES
TOKENS = 64
D = 3072
HID = 1024
MAXP = EP * CAP
BLOCK = YS * CAP
HEAD = 80
DYS = (0, 1, 3, 2)
GROUP = CORES * BLOCK
NEAR = 3 * GROUP
OWN = 32
STEP = 128
PLACED = 384
ORDER = ((0, 0), (1, 0), (3, 0), (0, 1), (1, 1), (3, 1), (2, 0), (2, 1))
VMEM = pl.BlockSpec(memory_space=pltpu.VMEM)
ANY = pl.BlockSpec(memory_space=pl.ANY)
HBM = pl.BlockSpec(memory_space=pltpu.HBM)
CHEAP = pl.CostEstimate(flops=1024, bytes_accessed=1024, transcendentals=0)
SOME = pl.CostEstimate(flops=1200 << 20, bytes_accessed=1024, transcendentals=0)
NT = (((1,), (1,)), ((), ()))


def hop(shard, dy=0, dx=0, dc=0):
    pairs = []
    for y in range(YS):
        for x in range(XS):
            for c in range(CORES):
                to = (((y + dy) % YS) * XS + (x + (dx, -dx)[c]) % XS) * CORES + (c + dc) % CORES
                pairs.append(((y * XS + x) * CORES + c, to))
    return lax.ppermute(shard, "ep", pairs)


def down(shard):
    n = lax.axis_size("section")
    return lax.ppermute(shard, "section", [(i, i - 1) for i in range(1, n)])


def front_kernel(moment, count, ids_hbm, share_hbm, router_hbm, gap_hbm, *refs):
    grads, outs = refs[:count], refs[-15:-8]
    ids_ref, share_ref, router_ref, gap_ref, grads_ref, parts_ref, departing_ref, sems = refs[-8:]
    pairs = [(ids_hbm.at[moment], ids_ref), (share_hbm, share_ref)]
    pairs += [(grads[i], grads_ref.at[i]) for i in range(count)]
    pairs += [(gap_hbm.at[moment], gap_ref), (router_hbm, router_ref)]
    loads = [pltpu.make_async_copy(source, to, sems.at[i]) for i, (source, to) in enumerate(pairs)]
    for load in loads:
        load.start()
    for load in loads[: 2 + count]:
        load.wait()
    me = lax.axis_index("ep")
    both = ids_ref[:, pl.ds(pl.multiple_of((me // 2) * 128, 128), 128)].astype(jnp.float32)
    own = jnp.where(me % 2 == 0, both[:, :TOKENS], both[:, TOKENS:])
    first, second = own[0:1], own[1:2]
    share = share_ref[moment : moment + 1, :]
    gradient = grads_ref[0]
    if count == 2:
        last = lax.axis_index("section") == lax.axis_size("section") - 1
        gradient = jnp.where(last, gradient, grads_ref[1])

    my_y = (me // (XS * CORES)).astype(jnp.float32)
    experts = lax.broadcasted_iota(jnp.int32, (8, TOKENS), 0).astype(jnp.float32)
    is_first, is_second = experts == first, experts == second
    chosen = (is_first | is_second).astype(jnp.float32).astype(jnp.bfloat16)
    rows = lax.broadcasted_iota(jnp.int32, (TOKENS, TOKENS), 0)
    columns = lax.broadcasted_iota(jnp.int32, (TOKENS, TOKENS), 1)
    before = (rows < columns).astype(jnp.float32).astype(jnp.bfloat16)
    ranks = jnp.dot(chosen, before, preferred_element_type=jnp.float32)

    def placed(expert, mask):
        relative = expert - my_y
        relative = jnp.where(relative < 0, relative + YS, relative)
        return relative * CAP + jnp.sum(jnp.where(mask, ranks, 0.0), 0, keepdims=True)

    place_1, place_2 = placed(first, is_first), placed(second, is_second)
    slots = lax.broadcasted_iota(jnp.int32, (CAP, TOKENS), 0).astype(jnp.float32)
    stores = []
    for j in range(YS):
        one, two = slots + j * CAP == place_1, slots + j * CAP == place_2
        weight = jnp.sum(jnp.where(one, share, 0.0) + jnp.where(two, 1.0 - share, 0.0), 1, keepdims=True)
        placing = (one | two).astype(jnp.float32).astype(jnp.bfloat16)
        gathered = jnp.dot(placing, gradient, preferred_element_type=jnp.float32)
        parts_ref[j] = (gathered * weight).astype(jnp.bfloat16)
        stores.append(pltpu.make_async_copy(parts_ref.at[j], outs[j], sems.at[4 + count + j]))
        stores[j].start()
    stores.append(pltpu.make_async_copy(parts_ref.at[0, pl.ds(0, OWN)], outs[YS], sems.at[4 + count + YS]))
    stores[YS].start()

    def upright(row):
        return jnp.sum(jnp.where(rows == columns, row, 0.0), 1, keepdims=True)

    for load in loads[2 + count :]:
        load.wait()
    first, second, share = upright(first), upright(second), upright(share)
    gradient = gradient.astype(jnp.float32)
    gap_dot = jnp.sum(gradient * gap_ref[...].astype(jnp.float32), 1, keepdims=True)
    logit_grad = share * (1.0 - share) * gap_dot
    term = jnp.zeros((TOKENS, D), jnp.float32)
    for e in range(YS):
        sign = jnp.where(first == e, 1.0, 0.0) - jnp.where(second == e, 1.0, 0.0)
        term = term + (logit_grad * sign) * router_ref[e : e + 1, :]
    departing_ref[...] = (gradient + term).astype(jnp.bfloat16)
    for to in (outs[YS + 1].at[moment], outs[YS + 2]):
        stores.append(pltpu.make_async_copy(departing_ref, to, sems.at[4 + count + len(stores)]))
        stores[-1].start()
    for store in stores:
        store.wait()


def front(moment, ids, share, router_rows, gap, grads, departs):
    more = [] if departs is None else [departs]
    count = len(grads)
    return pl.pallas_call(
        functools.partial(front_kernel, moment, count),
        out_shape=[jax.ShapeDtypeStruct((CAP, D), jnp.bfloat16)] * YS
        + [
            jax.ShapeDtypeStruct((OWN, D), jnp.bfloat16),
            jax.ShapeDtypeStruct((TICKS, TOKENS, D), jnp.bfloat16),
            jax.ShapeDtypeStruct((TOKENS, D), jnp.bfloat16),
        ],
        in_specs=[HBM] * (4 + count + len(more)),
        out_specs=[HBM] * (YS + 3),
        scratch_shapes=[
            pltpu.VMEM((2, EP * TOKENS), jnp.int32),
            pltpu.VMEM((TICKS, TOKENS), jnp.float32),
            pltpu.VMEM((YS, D), jnp.float32),
            pltpu.VMEM((TOKENS, D), jnp.bfloat16),
            pltpu.VMEM((count, TOKENS, D), jnp.bfloat16),
            pltpu.VMEM((YS, CAP, D), jnp.bfloat16),
            pltpu.VMEM((TOKENS, D), jnp.bfloat16),
            pltpu.SemaphoreType.DMA((4 + count + YS + 3,)),
        ],
        input_output_aliases={4 + count: YS + 1} if more else {},
        compiler_params=pltpu.CompilerParams(vmem_limit_bytes=60 << 20),
        cost_estimate=CHEAP,
        name="front",
    )(ids, share, router_rows, gap, *grads, *more)


def each(count, unrolled, body):
    if unrolled or count == 1:
        for k in range(count):
            body(k)
    else:
        pl.loop(0, count)(body)


def multiply(pieces, rows_ref, down_ref, product_ref, unrolled):
    begin = 0
    for piece in pieces:
        rows_ref[pl.ds(begin, piece.shape[0]), :] = piece[...]
        begin += piece.shape[0]

    def group(k):
        part = pl.ds(pl.multiple_of(k * GROUP, GROUP), GROUP)
        product = lax.dot_general(rows_ref[part, :], down_ref[...], NT, preferred_element_type=jnp.float32)
        product_ref[part, :] = product.astype(jnp.bfloat16)

    each(begin // GROUP, unrolled, group)


def plan_kernel(ids_ref, table_ref, *outs):
    me = lax.axis_index("ep")
    my_y, my_x, my_c = me // (XS * CORES), (me // CORES) % XS, me % CORES
    table = table_ref[...]
    source_c = (my_c - table[2:3]) & (CORES - 1)
    source_x = jnp.where(source_c == 0, my_x - table[1:2], my_x + table[1:2]) & (XS - 1)
    source = ((my_y - table[0:1]) & (YS - 1)) * (XS * CORES) + source_x * CORES + source_c
    slot = table[3:4].astype(jnp.float32)
    device = lax.broadcasted_iota(jnp.int32, (EP, MAXP), 0)
    ahead = (device < source).astype(jnp.float32).astype(jnp.bfloat16)
    itself = (device == source).astype(jnp.float32).astype(jnp.bfloat16)
    owner = lax.broadcasted_iota(jnp.int32, (EP, EP * TOKENS), 1) // TOKENS
    owned = (owner == lax.broadcasted_iota(jnp.int32, (EP, EP * TOKENS), 0)).astype(jnp.float32).astype(jnp.bfloat16)
    for moment in range(TICKS):
        named = (ids_ref[moment] == my_y).astype(jnp.float32)
        named = jnp.broadcast_to(named[0:1] + named[1:2], (8, EP * TOKENS)).astype(jnp.bfloat16)
        counts = lax.dot_general(named, owned, NT, preferred_element_type=jnp.float32).astype(jnp.bfloat16)
        offset = jnp.dot(counts, ahead, preferred_element_type=jnp.float32)[0:1]
        amount = jnp.dot(counts, itself, preferred_element_type=jnp.float32)[0:1]
        target = jnp.where(slot < amount, offset + slot, -1.0).astype(jnp.int32)

        for i, part in enumerate((target[:, :NEAR], target[:, NEAR:])):

            @pl.loop(0, MAXP // STEP)
            def _(k, out=outs[2 * moment + i], part=part):
                at = pl.multiple_of(k * STEP, STEP)
                here = lax.broadcasted_iota(jnp.int32, (STEP, part.shape[1]), 0) + at
                out[pl.ds(at, STEP), :] = (here == part).astype(jnp.float32).astype(jnp.bfloat16)


def plan(ids):
    columns = [(dy, dx, dc, slot) for dx, dc in ORDER for dy in DYS for slot in range(CAP)]
    table = np.zeros((8, MAXP), np.int32)
    table[:4] = np.array(columns, np.int32).T
    return pl.pallas_call(
        plan_kernel,
        out_shape=[jax.ShapeDtypeStruct((MAXP, n), jnp.bfloat16) for n in (NEAR, GROUP)] * TICKS,
        in_specs=[VMEM] * 2,
        out_specs=[VMEM] * (2 * TICKS),
        compiler_params=pltpu.CompilerParams(vmem_limit_bytes=16 << 20),
        cost_estimate=CHEAP,
        name="plan",
    )(ids, jnp.asarray(table))


def near_kernel(count, unrolled, placing_ref, down_ref, *refs):
    out_ref, rows_ref, product_ref = refs[count:]
    multiply(refs[:count], rows_ref, down_ref, product_ref, unrolled)

    def place(k):
        part = pl.ds(pl.multiple_of(k * PLACED, PLACED), PLACED)
        placed = jnp.dot(placing_ref[part, :], product_ref[...], preferred_element_type=jnp.float32)
        out_ref[part, :] = placed.astype(jnp.bfloat16)

    each(MAXP // PLACED, unrolled, place)


def near_product(placing, pieces, down_rows, unrolled):
    return pl.pallas_call(
        functools.partial(near_kernel, len(pieces), unrolled),
        out_shape=jax.ShapeDtypeStruct((MAXP, HID), jnp.bfloat16),
        in_specs=[VMEM] * (2 + len(pieces)),
        out_specs=VMEM,
        scratch_shapes=[
            pltpu.VMEM((NEAR, D), jnp.bfloat16),
            pltpu.VMEM((NEAR, HID), jnp.bfloat16),
        ],
        compiler_params=pltpu.CompilerParams(vmem_limit_bytes=24 << 20),
        cost_estimate=CHEAP,
        name="near_product",
    )(placing, down_rows, *pieces)


def far_kernel(moment, count, placing_ref, down_ref, near_ref, *refs):
    out_ref, rows_ref, product_ref, placed_ref, sems = refs[-5:]
    multiply(refs[:count], rows_ref, down_ref, product_ref, True)
    stores = []
    for k in range(MAXP // PLACED):
        part = pl.ds(k * PLACED, PLACED)
        placed = jnp.dot(placing_ref[part, :], product_ref[...], preferred_element_type=jnp.float32)
        placed_ref[part, :] = (placed + near_ref[part, :].astype(jnp.float32)).astype(jnp.bfloat16)
        stores.append(pltpu.make_async_copy(placed_ref.at[part], out_ref.at[moment, part], sems.at[k]))
        stores[k].start()
    for store in stores:
        store.wait()


def far_product(moment, placing, pieces, near, down_rows, hidden):
    more = [] if hidden is None else [hidden]
    return pl.pallas_call(
        functools.partial(far_kernel, moment, len(pieces)),
        out_shape=jax.ShapeDtypeStruct((TICKS, MAXP, HID), jnp.bfloat16),
        in_specs=[VMEM] * (3 + len(pieces)) + [ANY] * len(more),
        out_specs=ANY,
        scratch_shapes=[
            pltpu.VMEM((GROUP, D), jnp.bfloat16),
            pltpu.VMEM((GROUP, HID), jnp.bfloat16),
            pltpu.VMEM((MAXP, HID), jnp.bfloat16),
            pltpu.SemaphoreType.DMA((MAXP // PLACED,)),
        ],
        input_output_aliases={3 + len(pieces): 0} if more else {},
        compiler_params=pltpu.CompilerParams(vmem_limit_bytes=24 << 20),
        cost_estimate=SOME,
        name="far_product",
    )(placing, down_rows, near, *pieces, *more)


def spread(parts):
    return {j: hop(parts[j], dy=j) for j in (1, 3, 2)}


def joined(own, came):
    return jnp.concatenate([own, came[1], came[3], came[2]], 0)


def swapped(tree):
    return jax.tree.map(lambda p: hop(p, dc=1), tree)


def local(arriving, top_grad, expert_ids, first_share, out_gap, router_weight, down_weight):
    tie = lax.optimization_barrier
    ids = jnp.swapaxes(expert_ids[0], 1, 2)
    share, gap, router_rows, down_rows = first_share[0], out_gap[0], router_weight[0], down_weight[0]

    *parts0, head0, departs, departing = front(0, ids, share, router_rows, gap, [arriving[0]], None)
    grads = [top_grad[0], down(departing)]
    *parts1, _, departs, _ = front(1, ids, share, router_rows, gap, grads, departs)
    first0 = hop(head0, dx=1)
    own0, came0, first0, parts1, departs = tie((parts0[0], spread(parts0), first0, parts1, departs))

    block0 = joined(own0, came0)
    near0 = {1: [first0, hop(block0[OWN:], dx=1)], 3: [hop(block0, dx=3)]}
    placing = plan(ids)
    own1, came1, block0, near0, placing = tie((parts1[0], spread(parts1), block0, near0, placing))

    block1 = joined(own1, came1)
    far0 = hop(near0[3][0], dx=3)
    near1 = {dx: [hop(block1, dx=dx)] for dx in (1, 3)}
    pieces = [block0, *near0[1], *near0[3]]
    product0 = near_product(placing[0], [*pieces, swapped(jnp.concatenate(pieces))], down_rows, False)
    far0, product0 = tie((far0, product0))
    hidden = far_product(0, placing[1], [far0, *swapped([far0[:HEAD], far0[HEAD:]])], product0, down_rows, None)
    block1, near1, hidden = tie((block1, near1, hidden))

    far1 = hop(near1[1][0], dx=1)
    pieces = [block1, *near1[1], *near1[3]]
    product1 = near_product(placing[2], [*pieces, swapped(jnp.concatenate(pieces))], down_rows, True)
    far1, product1 = tie((far1, product1))

    hidden = far_product(1, placing[3], [far1, swapped(far1)], product1, down_rows, hidden)
    return departs[None], hidden[None]


def solution(mesh):
    placed = (
        P("section", "ep", None),
        P(None, "ep", None),
        P("section", None, None, None),
        P("section", None, "ep"),
        P("section", None, "ep", None),
        P("section", None, None),
        P("section", "ep", None),
    )
    return jax.shard_map(
        local,
        mesh=mesh,
        in_specs=placed,
        out_specs=(P("section", None, "ep", None), P("section", None, "ep", None)),
        check_vma=False,
    )
```

```python
import functools

import jax
import jax.numpy as jnp
import numpy as np
from jax import lax
from jax.experimental import pallas as pl
from jax.experimental.pallas import tpu as pltpu
from jax.sharding import PartitionSpec as P

TICKS = 2
CAP = 36
XS, YS, CORES = 4, 4, 2
EP = XS * YS * CORES
TOKENS = 64
D = 3072
HID = 1024
MAXP = EP * CAP
BLOCK = YS * CAP
HEAD = 80
DYS = (0, 1, 3, 2)
GROUP = CORES * BLOCK
PART = 112
NEAR = 3 * GROUP
OWN = 32
STEP = 128
PLACED = 384
ORDER = ((0, 0), (1, 0), (3, 0), (0, 1), (1, 1), (3, 1), (2, 0), (2, 1))
VMEM = pl.BlockSpec(memory_space=pltpu.VMEM)
ANY = pl.BlockSpec(memory_space=pl.ANY)
HBM = pl.BlockSpec(memory_space=pltpu.HBM)
CHEAP = pl.CostEstimate(flops=1024, bytes_accessed=1024, transcendentals=0)
SOME = pl.CostEstimate(flops=1200 << 20, bytes_accessed=1024, transcendentals=0)
NT = (((1,), (1,)), ((), ()))


def hop(shard, dy=0, dx=0, dc=0):
    pairs = []
    for y in range(YS):
        for x in range(XS):
            for c in range(CORES):
                to = (((y + dy) % YS) * XS + (x + (dx, -dx)[c]) % XS) * CORES + (c + dc) % CORES
                pairs.append(((y * XS + x) * CORES + c, to))
    return lax.ppermute(shard, "ep", pairs)


def down(shard):
    n = lax.axis_size("section")
    return lax.ppermute(shard, "section", [(i, i - 1) for i in range(1, n)])


def front_kernel(moment, count, ids_hbm, share_hbm, router_hbm, gap_hbm, *refs):
    grads, outs = refs[:count], refs[-15:-8]
    ids_ref, share_ref, router_ref, gap_ref, grads_ref, parts_ref, departing_ref, sems = refs[-8:]
    pairs = [(ids_hbm.at[moment], ids_ref), (share_hbm, share_ref)]
    pairs += [(grads[i], grads_ref.at[i]) for i in range(count)]
    pairs += [(gap_hbm.at[moment], gap_ref), (router_hbm, router_ref)]
    loads = [pltpu.make_async_copy(source, to, sems.at[i]) for i, (source, to) in enumerate(pairs)]
    for load in loads:
        load.start()
    for load in loads[: 2 + count]:
        load.wait()
    me = lax.axis_index("ep")
    both = ids_ref[:, pl.ds(pl.multiple_of((me // 2) * 128, 128), 128)].astype(jnp.float32)
    own = jnp.where(me % 2 == 0, both[:, :TOKENS], both[:, TOKENS:])
    first, second = own[0:1], own[1:2]
    share = share_ref[moment : moment + 1, :]
    gradient = grads_ref[0]
    if count == 2:
        last = lax.axis_index("section") == lax.axis_size("section") - 1
        gradient = jnp.where(last, gradient, grads_ref[1])

    my_y = (me // (XS * CORES)).astype(jnp.float32)
    experts = lax.broadcasted_iota(jnp.int32, (8, TOKENS), 0).astype(jnp.float32)
    is_first, is_second = experts == first, experts == second
    chosen = (is_first | is_second).astype(jnp.float32).astype(jnp.bfloat16)
    rows = lax.broadcasted_iota(jnp.int32, (TOKENS, TOKENS), 0)
    columns = lax.broadcasted_iota(jnp.int32, (TOKENS, TOKENS), 1)
    before = (rows < columns).astype(jnp.float32).astype(jnp.bfloat16)
    ranks = jnp.dot(chosen, before, preferred_element_type=jnp.float32)

    def placed(expert, mask):
        relative = expert - my_y
        relative = jnp.where(relative < 0, relative + YS, relative)
        return relative * CAP + jnp.sum(jnp.where(mask, ranks, 0.0), 0, keepdims=True)

    place_1, place_2 = placed(first, is_first), placed(second, is_second)
    slots = lax.broadcasted_iota(jnp.int32, (CAP, TOKENS), 0).astype(jnp.float32)
    stores = []
    for j in range(YS):
        one, two = slots + j * CAP == place_1, slots + j * CAP == place_2
        weight = jnp.sum(jnp.where(one, share, 0.0) + jnp.where(two, 1.0 - share, 0.0), 1, keepdims=True)
        placing = (one | two).astype(jnp.float32).astype(jnp.bfloat16)
        gathered = jnp.dot(placing, gradient, preferred_element_type=jnp.float32)
        parts_ref[j] = (gathered * weight).astype(jnp.bfloat16)
        stores.append(pltpu.make_async_copy(parts_ref.at[j], outs[j], sems.at[4 + count + j]))
        stores[j].start()
    stores.append(pltpu.make_async_copy(parts_ref.at[0, pl.ds(0, OWN)], outs[YS], sems.at[4 + count + YS]))
    stores[YS].start()

    def upright(row):
        return jnp.sum(jnp.where(rows == columns, row, 0.0), 1, keepdims=True)

    for load in loads[2 + count :]:
        load.wait()
    first, second, share = upright(first), upright(second), upright(share)
    gradient = gradient.astype(jnp.float32)
    gap_dot = jnp.sum(gradient * gap_ref[...].astype(jnp.float32), 1, keepdims=True)
    logit_grad = share * (1.0 - share) * gap_dot
    term = jnp.zeros((TOKENS, D), jnp.float32)
    for e in range(YS):
        sign = jnp.where(first == e, 1.0, 0.0) - jnp.where(second == e, 1.0, 0.0)
        term = term + (logit_grad * sign) * router_ref[e : e + 1, :]
    departing_ref[...] = (gradient + term).astype(jnp.bfloat16)
    for to in (outs[YS + 1].at[moment], outs[YS + 2]):
        stores.append(pltpu.make_async_copy(departing_ref, to, sems.at[4 + count + len(stores)]))
        stores[-1].start()
    for store in stores:
        store.wait()


def front(moment, ids, share, router_rows, gap, grads, departs):
    more = [] if departs is None else [departs]
    count = len(grads)
    return pl.pallas_call(
        functools.partial(front_kernel, moment, count),
        out_shape=[jax.ShapeDtypeStruct((CAP, D), jnp.bfloat16)] * YS
        + [
            jax.ShapeDtypeStruct((OWN, D), jnp.bfloat16),
            jax.ShapeDtypeStruct((TICKS, TOKENS, D), jnp.bfloat16),
            jax.ShapeDtypeStruct((TOKENS, D), jnp.bfloat16),
        ],
        in_specs=[HBM] * (4 + count + len(more)),
        out_specs=[HBM] * (YS + 3),
        scratch_shapes=[
            pltpu.VMEM((2, EP * TOKENS), jnp.int32),
            pltpu.VMEM((TICKS, TOKENS), jnp.float32),
            pltpu.VMEM((YS, D), jnp.float32),
            pltpu.VMEM((TOKENS, D), jnp.bfloat16),
            pltpu.VMEM((count, TOKENS, D), jnp.bfloat16),
            pltpu.VMEM((YS, CAP, D), jnp.bfloat16),
            pltpu.VMEM((TOKENS, D), jnp.bfloat16),
            pltpu.SemaphoreType.DMA((4 + count + YS + 3,)),
        ],
        input_output_aliases={4 + count: YS + 1} if more else {},
        compiler_params=pltpu.CompilerParams(vmem_limit_bytes=60 << 20),
        cost_estimate=CHEAP,
        name="front",
    )(ids, share, router_rows, gap, *grads, *more)


def each(count, unrolled, body):
    if unrolled or count == 1:
        for k in range(count):
            body(k)
    else:
        pl.loop(0, count)(body)


def multiply(pieces, rows_ref, down_ref, product_ref, unrolled):
    begin = 0
    for piece in pieces:
        rows_ref[pl.ds(begin, piece.shape[0]), :] = piece[...]
        begin += piece.shape[0]

    def group(k):
        part = pl.ds(pl.multiple_of(k * GROUP, GROUP), GROUP)
        product = lax.dot_general(rows_ref[part, :], down_ref[...], NT, preferred_element_type=jnp.float32)
        product_ref[part, :] = product.astype(jnp.bfloat16)

    each(begin // GROUP, unrolled, group)


def plan_kernel(ids_ref, table_ref, *outs):
    me = lax.axis_index("ep")
    my_y, my_x, my_c = me // (XS * CORES), (me // CORES) % XS, me % CORES
    table = table_ref[...]
    source_c = (my_c - table[2:3]) & (CORES - 1)
    source_x = jnp.where(source_c == 0, my_x - table[1:2], my_x + table[1:2]) & (XS - 1)
    source = ((my_y - table[0:1]) & (YS - 1)) * (XS * CORES) + source_x * CORES + source_c
    slot = table[3:4].astype(jnp.float32)
    device = lax.broadcasted_iota(jnp.int32, (EP, MAXP), 0)
    ahead = (device < source).astype(jnp.float32).astype(jnp.bfloat16)
    itself = (device == source).astype(jnp.float32).astype(jnp.bfloat16)
    owner = lax.broadcasted_iota(jnp.int32, (EP, EP * TOKENS), 1) // TOKENS
    owned = (owner == lax.broadcasted_iota(jnp.int32, (EP, EP * TOKENS), 0)).astype(jnp.float32).astype(jnp.bfloat16)
    for moment in range(TICKS):
        named = (ids_ref[moment] == my_y).astype(jnp.float32)
        named = jnp.broadcast_to(named[0:1] + named[1:2], (8, EP * TOKENS)).astype(jnp.bfloat16)
        counts = lax.dot_general(named, owned, NT, preferred_element_type=jnp.float32).astype(jnp.bfloat16)
        offset = jnp.dot(counts, ahead, preferred_element_type=jnp.float32)[0:1]
        amount = jnp.dot(counts, itself, preferred_element_type=jnp.float32)[0:1]
        target = jnp.where(slot < amount, offset + slot, -1.0).astype(jnp.int32)

        for i, part in enumerate((target[:, :NEAR], target[:, NEAR:])):

            @pl.loop(0, MAXP // STEP)
            def _(k, out=outs[2 * moment + i], part=part):
                at = pl.multiple_of(k * STEP, STEP)
                here = lax.broadcasted_iota(jnp.int32, (STEP, part.shape[1]), 0) + at
                out[pl.ds(at, STEP), :] = (here == part).astype(jnp.float32).astype(jnp.bfloat16)


def plan(ids):
    columns = [(dy, dx, dc, slot) for dx, dc in ORDER for dy in DYS for slot in range(CAP)]
    table = np.zeros((8, MAXP), np.int32)
    table[:4] = np.array(columns, np.int32).T
    return pl.pallas_call(
        plan_kernel,
        out_shape=[jax.ShapeDtypeStruct((MAXP, n), jnp.bfloat16) for n in (NEAR, GROUP)] * TICKS,
        in_specs=[VMEM] * 2,
        out_specs=[VMEM] * (2 * TICKS),
        compiler_params=pltpu.CompilerParams(vmem_limit_bytes=16 << 20),
        cost_estimate=CHEAP,
        name="plan",
    )(ids, jnp.asarray(table))


def near_kernel(count, unrolled, placing_ref, down_ref, *refs):
    out_ref, rows_ref, product_ref = refs[count:]
    multiply(refs[:count], rows_ref, down_ref, product_ref, unrolled)

    def place(k):
        part = pl.ds(pl.multiple_of(k * PLACED, PLACED), PLACED)
        placed = jnp.dot(placing_ref[part, :], product_ref[...], preferred_element_type=jnp.float32)
        out_ref[part, :] = placed.astype(jnp.bfloat16)

    each(MAXP // PLACED, unrolled, place)


def near_product(placing, pieces, down_rows, unrolled):
    return pl.pallas_call(
        functools.partial(near_kernel, len(pieces), unrolled),
        out_shape=jax.ShapeDtypeStruct((MAXP, HID), jnp.bfloat16),
        in_specs=[VMEM] * (2 + len(pieces)),
        out_specs=VMEM,
        scratch_shapes=[
            pltpu.VMEM((NEAR, D), jnp.bfloat16),
            pltpu.VMEM((NEAR, HID), jnp.bfloat16),
        ],
        compiler_params=pltpu.CompilerParams(vmem_limit_bytes=24 << 20),
        cost_estimate=CHEAP,
        name="near_product",
    )(placing, down_rows, *pieces)


def far_kernel(moment, count, placing_ref, down_ref, near_ref, *refs):
    out_ref, rows_ref, product_ref, placed_ref, sems = refs[-5:]
    multiply(refs[:count], rows_ref, down_ref, product_ref, True)
    stores = []
    for k in range(MAXP // PLACED):
        part = pl.ds(k * PLACED, PLACED)
        placed = jnp.dot(placing_ref[part, :], product_ref[...], preferred_element_type=jnp.float32)
        placed_ref[part, :] = (placed + near_ref[part, :].astype(jnp.float32)).astype(jnp.bfloat16)
        stores.append(pltpu.make_async_copy(placed_ref.at[part], out_ref.at[moment, part], sems.at[k]))
        stores[k].start()
    for store in stores:
        store.wait()


def far_product(moment, placing, pieces, near, down_rows, hidden):
    more = [] if hidden is None else [hidden]
    return pl.pallas_call(
        functools.partial(far_kernel, moment, len(pieces)),
        out_shape=jax.ShapeDtypeStruct((TICKS, MAXP, HID), jnp.bfloat16),
        in_specs=[VMEM] * (3 + len(pieces)) + [ANY] * len(more),
        out_specs=ANY,
        scratch_shapes=[
            pltpu.VMEM((GROUP, D), jnp.bfloat16),
            pltpu.VMEM((GROUP, HID), jnp.bfloat16),
            pltpu.VMEM((MAXP, HID), jnp.bfloat16),
            pltpu.SemaphoreType.DMA((MAXP // PLACED,)),
        ],
        input_output_aliases={3 + len(pieces): 0} if more else {},
        compiler_params=pltpu.CompilerParams(vmem_limit_bytes=24 << 20),
        cost_estimate=SOME,
        name="far_product",
    )(placing, down_rows, near, *pieces, *more)


def spread(parts):
    return {j: hop(parts[j], dy=j) for j in (1, 3, 2)}


def joined(own, came):
    return jnp.concatenate([own, came[1], came[3], came[2]], 0)


def swapped(tree):
    return jax.tree.map(lambda p: hop(p, dc=1), tree)


def local(arriving, top_grad, expert_ids, first_share, out_gap, router_weight, down_weight):
    tie = lax.optimization_barrier
    ids = jnp.swapaxes(expert_ids[0], 1, 2)
    share, gap, router_rows, down_rows = first_share[0], out_gap[0], router_weight[0], down_weight[0]

    *parts0, head0, departs, departing = front(0, ids, share, router_rows, gap, [arriving[0]], None)
    grads = [top_grad[0], down(departing)]
    *parts1, _, departs, _ = front(1, ids, share, router_rows, gap, grads, departs)
    first0 = hop(head0, dx=1)
    own0, came0, first0, parts1, departs = tie((parts0[0], spread(parts0), first0, parts1, departs))

    block0 = joined(own0, came0)
    near0 = {1: [first0, hop(block0[OWN:], dx=1)], 3: [hop(block0, dx=3)]}
    placing = plan(ids)
    own1, came1, block0, near0, placing = tie((parts1[0], spread(parts1), block0, near0, placing))

    block1 = joined(own1, came1)
    far0 = hop(near0[3][0], dx=3)
    near1 = {dx: [hop(block1, dx=dx)] for dx in (1, 3)}
    pieces = [block0, *near0[1], *near0[3]]
    product0 = near_product(placing[0], [*pieces, swapped(jnp.concatenate(pieces))], down_rows, False)
    far0, product0 = tie((far0, product0))
    hidden = far_product(0, placing[1], [far0, *swapped([far0[:HEAD], far0[HEAD:]])], product0, down_rows, None)
    block1, near1, hidden = tie((block1, near1, hidden))

    far1 = hop(near1[1][0], dx=1)
    pieces = [block1, *near1[1], *near1[3]]
    chunks = [jnp.concatenate(pieces)[at : at + PART] for at in range(0, 3 * BLOCK, PART)]
    product1 = near_product(placing[2], [*pieces, *swapped(chunks)], down_rows, True)
    far1, product1 = tie((far1, product1))

    hidden = far_product(1, placing[3], [far1, swapped(far1)], product1, down_rows, hidden)
    return departs[None], hidden[None]


def solution(mesh):
    placed = (
        P("section", "ep", None),
        P(None, "ep", None),
        P("section", None, None, None),
        P("section", None, "ep"),
        P("section", None, "ep", None),
        P("section", None, None),
        P("section", "ep", None),
    )
    return jax.shard_map(
        local,
        mesh=mesh,
        in_specs=placed,
        out_specs=(P("section", None, "ep", None), P("section", None, "ep", None)),
        check_vma=False,
    )
```
